32 devices in a mesh: gx: 4 (over x, core), gy: 8 (over z, y).
Axes of the slice: x: 2, y: 2, z: 4, core: 2. Of those that a mesh axis runs over, the one named last changes fastest.
Arguments:
- multipoles: bfloat16 [165, 8192], P(None, ('gx', 'gy')), may hold values from -6 to 6
- operators: bfloat16 [64, 165, 165], replicated, may hold values from -0.125 to 0.125
- boundary: int32 [5, 4096], P(None, ('gx', 'gy')), may hold values from 0 to 767, as said below
- pair_target: int32 [64, 4096], P(None, ('gx', 'gy')), may hold values from 0 to 255
- pair_source: int32 [64, 4096], P(None, ('gx', 'gy')), may hold values from 0 to 895
- pair_count: int32 [64, 32], P(None, ('gx', 'gy')), may hold values from 1 to 128, as said below
Outputs:
- local_expansions: float32 [165, 8192], P(None, ('gx', 'gy'))
The draws below stay inside these ranges and needn't reach their ends.
Inputs may be any that keep to these rules, and one draw needn't show every extreme that they name: `boundary`: on every device and cut l, the list holds 128 distinct columns in increasing order, all below 256 + l * 128, and always includes column 256 + l * 128 - 1. `pair_count`: on every device, some class uses all 128 slots.
All inputs are finite; a program needn't handle non-finite values.
Results may differ from the reference program's by a relative error of at most 0.0003.
Values may be sent and summed in bfloat16 or wider, within the bound.
No kernel may reach another device: no remote copies, remote signals or barrier semaphores. Data moves between devices by JAX's collectives and lax.ppermute only.
A program may use at most 64 MiB of HBM per device.

```python
import jax
import jax.numpy as jnp
from jax import lax

P_SIZE = 165
NCLASS = 64
CELLS = 256
NB = 128
W = 128
LEVELS = 5
POOL = 896
DEVICES = 32


def draw_boundary(key, part):
    width = CELLS + (LEVELS - 1) * NB
    scores = jax.random.randint(key, (LEVELS, DEVICES, width), 0, 1 << 18)
    column = jnp.arange(width, dtype=jnp.int32)
    column_limit = CELLS + jnp.arange(LEVELS, dtype=jnp.int32) * NB
    ranked_scores = scores * width + column[None, None, :]
    ranked_scores = jnp.where(column[None, None, :] < column_limit[:, None, None] - 1, ranked_scores, -1)
    ranked_scores = jnp.where(column[None, None, :] == column_limit[:, None, None] - 1, (1 << 18) * width + width, ranked_scores)
    _, chosen = lax.top_k(ranked_scores, NB)
    chosen = jnp.sort(chosen, axis=-1)
    return chosen.reshape(LEVELS, DEVICES * NB).astype(jnp.int32)


def draw_pair_count(key, part):
    first_key = jax.random.fold_in(key, 11)
    second_key = jax.random.fold_in(key, 12)
    counts = jax.random.randint(first_key, (NCLASS, DEVICES), 1, W + 1)
    full_class = jax.random.randint(second_key, (DEVICES,), 0, NCLASS)
    class_ids = jnp.arange(NCLASS, dtype=jnp.int32)
    counts = jnp.where(class_ids[:, None] == full_class[None, :], W, counts)
    return counts.astype(jnp.int32)


def touch_ends(entries, key, low, largest):
    place = [jax.random.randint(jax.random.fold_in(key, axis), (), 0, length) for axis, length in enumerate(entries.shape)]
    longest = entries.shape.index(max(entries.shape))
    neighbour = place[:longest] + [(place[longest] + 1) % entries.shape[longest]] + place[longest + 1:]
    return entries.at[tuple(place)].set(low).at[tuple(neighbour)].set(largest)


def levels(own_key, shape, cuts, least, largest):
    def one(position, blocks):
        draws = jax.random.uniform(jax.random.fold_in(jax.random.fold_in(own_key, 6), position), (blocks,), jnp.float32, least / len(cuts), largest / len(cuts))
        return jnp.repeat(jnp.exp(draws), shape[position] // blocks).reshape((-1,) + (1,) * (len(shape) - position - 1))

    gain = one(*cuts[0])
    for cut in cuts[1:]:
        gain = gain * one(*cut)
    return gain


def bell_draw(own_key, shape, deviation, limit, shards=(), kind=jnp.bfloat16):
    array = jax.random.normal(own_key, shape, jnp.float32) * deviation
    if len(shards) > 0:
        array = levels(own_key, shape, shards, -0.22, 0.18) * array
    return jnp.clip(array, min=-limit, max=limit).astype(kind)


def setup_inputs(seed: int = 0) -> dict:
    splits = jax.random.split(jax.random.key(seed), 7)
    return {
        "multipoles": bell_draw(splits[0], (P_SIZE, CELLS * DEVICES), 1.0, 6.0, ((1, 32),)),
        "operators": bell_draw(splits[1], (NCLASS, P_SIZE, P_SIZE), (16 * P_SIZE) ** -0.5, 0.125),
        "boundary": draw_boundary(jax.random.fold_in(splits[6], 71), 0),
        "pair_target": touch_ends(jax.random.randint(splits[3], (NCLASS, W * DEVICES), 0, CELLS), jax.random.fold_in(splits[3], 1), 0, CELLS - 1).astype(jnp.int32),
        "pair_source": touch_ends(jax.random.randint(splits[4], (NCLASS, W * DEVICES), 0, POOL), jax.random.fold_in(splits[4], 1), 0, POOL - 1).astype(jnp.int32),
        "pair_count": draw_pair_count(jax.random.fold_in(splits[6], 71), 0),
    }


def reference(multipoles, operators, boundary, pair_target, pair_source, pair_count):
    device_ids = jnp.arange(DEVICES, dtype=jnp.int32)
    anchor = device_ids[:, None] * CELLS + jnp.arange(CELLS, dtype=jnp.int32)[None, :]
    cut_lists = boundary.reshape(LEVELS, DEVICES, NB)
    for cut_level in range(LEVELS):
        partner = device_ids ^ (1 << (LEVELS - 1 - cut_level))
        exported = jnp.take_along_axis(anchor, cut_lists[cut_level], axis=1)
        anchor = jnp.concatenate([anchor, exported[partner]], axis=1).astype(jnp.int32)
    multipole_wide = multipoles.astype(jnp.float32)
    operator_wide = operators.astype(jnp.float32)
    targets = pair_target.reshape(NCLASS, DEVICES, W).transpose(1, 0, 2)
    sources = pair_source.reshape(NCLASS, DEVICES, W).transpose(1, 0, 2)
    counts = pair_count.T
    slot_ids = jnp.arange(W, dtype=jnp.int32)

    def device_step(expansions, pieces):
        device, anchor_ids, target_rows, source_rows, device_counts = pieces
        active = slot_ids[None, :] < device_counts[:, None]
        source_ids = anchor_ids[source_rows].astype(jnp.int32)
        target_ids = (device * CELLS + target_rows).astype(jnp.int32)
        gathered = jnp.take(multipole_wide, source_ids, axis=1)
        forward_terms = jnp.einsum("cij,jcs->ics", operator_wide, gathered)
        forward_terms = jnp.where(active[None], forward_terms, 0.0)
        own_columns = jnp.take(multipole_wide, target_ids[::-1], axis=1)
        reverse_terms = jnp.einsum("cij,jcs->ics", operator_wide, own_columns)
        reverse_terms = jnp.where(active[::-1][None], reverse_terms, 0.0)
        destinations = jnp.concatenate([target_ids, source_ids[::-1]], axis=1).reshape(-1)
        all_terms = jnp.concatenate([forward_terms, reverse_terms], axis=2).reshape(P_SIZE, -1)
        return expansions.at[:, destinations].add(all_terms), None

    start = jnp.zeros((P_SIZE, DEVICES * CELLS), jnp.float32)
    expansions, _ = lax.scan(device_step, start, (device_ids, anchor, targets, sources, counts))
    return expansions
```

```python
import jax
import jax.numpy as jnp
from jax import lax
from jax.experimental import pallas as pl
from jax.experimental.pallas import tpu as pltpu
from jax.sharding import PartitionSpec as P

LANES = 128
GROUP = 4
VMEM = pl.BlockSpec(memory_space=pltpu.VMEM)


def from_partner(block, axes, distance):
    count = lax.axis_size(axes)
    route = []
    for low in range(count):
        high = low | 1 << distance
        if high != low and high < count:
            route += [(low, high), (high, low)]
    return lax.ppermute(block, axes, route)


def one_hot(row, first, height):
    blocks = []
    for low in range(0, height, LANES):
        near = (row - (first + low)).astype(jnp.float32).astype(jnp.bfloat16)
        place = lax.broadcasted_iota(jnp.int32, (LANES, row.shape[1]), 0)
        place = place.astype(jnp.float32).astype(jnp.bfloat16)
        blocks.append(jnp.where(place == near, 1.0, 0.0).astype(jnp.bfloat16))
    return jnp.concatenate(blocks, axis=0) if len(blocks) > 1 else blocks[0]


def halves(wide):
    high = wide.astype(jnp.bfloat16)
    low = (wide - high.astype(jnp.float32)).astype(jnp.bfloat16)
    return high, low


def dot(a, b):
    return jnp.dot(a, b, preferred_element_type=jnp.float32)


def dot_nt(a, b):
    return lax.dot_general(a, b, (((1,), (1,)), ((), ())), preferred_element_type=jnp.float32)


def move(values, hot, how):
    high, low = halves(values)
    return how(high, hot) + how(low, hot)


def rows_of(ref, classes):
    return jnp.concatenate([ref[i] for i in range(classes)], axis=1)


def reverse_kernel(starts, mult_ref, op_ref, target_ref, source_ref, *refs):
    outs, total = refs[:-1], refs[-1]
    step = pl.program_id(0)
    group = op_ref.shape[0]
    cells = mult_ref.shape[1]

    @pl.when(step == 0)
    def _():
        total[...] = jnp.zeros_like(total)

    targets = rows_of(target_ref, group)
    sources = rows_of(source_ref, group)
    own = dot(mult_ref[...], one_hot(targets, 0, cells)).astype(jnp.bfloat16)
    width = targets.shape[1] // group
    terms = [
        dot(op_ref[group - 1 - i], own[:, i * width : (i + 1) * width]) for i in range(group)
    ]
    high, low = halves(jnp.concatenate(terms, axis=1))
    hot = one_hot(sources, 0, total.shape[1])
    total[...] += dot_nt(high, hot) + dot_nt(low, hot)

    @pl.when(step == pl.num_programs(0) - 1)
    def _():
        for out, first in zip(outs, starts):
            out[...] = total[:, first : first + out.shape[1]]


def forward_kernel(starts, *refs):
    segs = refs[: len(starts)]
    op_ref, target_ref, source_ref, out_ref, pool = refs[len(starts) :]
    step = pl.program_id(0)
    group = op_ref.shape[0]

    @pl.when(step == 0)
    def _():
        out_ref[...] = jnp.zeros_like(out_ref)
        for seg, first in zip(segs, starts):
            pool[:, first : first + seg.shape[1]] = seg[...]

    targets = rows_of(target_ref, group)
    sources = rows_of(source_ref, group)
    taken = dot(pool[...], one_hot(sources, 0, pool.shape[1])).astype(jnp.bfloat16)
    width = targets.shape[1] // group
    terms = [dot(op_ref[i], taken[:, i * width : (i + 1) * width]) for i in range(group)]
    high, low = halves(jnp.concatenate(terms, axis=1))
    hot = one_hot(targets, 0, out_ref.shape[1])
    out_ref[...] += dot_nt(high, hot) + dot_nt(low, hot)


def export_kernel(starts, list_ref, *refs):
    segs, out_ref = refs[:-1], refs[-1]
    row = list_ref[...]
    out = 0.0
    for seg, first in zip(segs, starts):
        out = out + dot(seg[...], one_hot(row, first, seg.shape[1]))
    out_ref[...] = out.astype(jnp.bfloat16)


def return_kernel(first, bases, lists_ref, *refs):
    out_ref = refs[-1]
    returned = refs[bases:-1]
    width = out_ref.shape[1]
    out = refs[0][...]
    for ref in refs[1:bases]:
        out = out + ref[...]
    cut = lists_ref.shape[0] - len(returned)
    for i, ref in enumerate(returned):
        hot = one_hot(lists_ref[cut + i : cut + i + 1, :], first, width)
        out = out + move(ref[...], hot, dot_nt)
    out_ref[...] = out


def call(kernel, out_shape, args, **more):
    return pl.pallas_call(
        kernel,
        out_shape=out_shape,
        in_specs=[VMEM] * len(args),
        out_specs=VMEM,
        **more,
    )(*args)


def per_device(multipoles, operators, boundary, pair_target, pair_source, pair_count):
    coefficients, cells = multipoles.shape
    cuts, sent = boundary.shape
    classes, width = pair_target.shape
    starts = [0] + [cells + cut * sent for cut in range(cuts)]
    sizes = [cells] + [sent] * cuts
    pool_width = cells + cuts * sent
    axes = ("gx", "gy")
    group = GROUP if classes % GROUP == 0 else 1
    steps = classes // group

    active = lax.broadcasted_iota(jnp.int32, pair_target.shape, 1) < pair_count
    source = jnp.where(active, pair_source, -1).reshape(classes, 1, width)
    target = pair_target.reshape(classes, 1, width)

    def whole(rows, columns):
        return pl.BlockSpec((rows, columns), lambda i: (0, 0))

    row_spec = pl.BlockSpec((group, 1, width), lambda i: (i, 0, 0))
    params = pltpu.CompilerParams(vmem_limit_bytes=48 * 1024 * 1024)
    flops = 2 * classes * width * coefficients * (pool_width * 2 + cells + coefficients)
    cost = pl.CostEstimate(flops=flops, bytes_accessed=operators.size * 2, transcendentals=0)

    def f_shape(columns):
        return jax.ShapeDtypeStruct((coefficients, columns), jnp.float32)

    def reverse_body(*refs):
        reverse_kernel(starts, *refs)

    with jax.named_scope("reverse_terms"):
        expansions = pl.pallas_call(
            reverse_body,
            grid=(steps,),
            in_specs=[
                whole(coefficients, cells),
                pl.BlockSpec((group, coefficients, coefficients), lambda i: (steps - 1 - i, 0, 0)),
                row_spec,
                row_spec,
            ],
            out_specs=[whole(coefficients, size) for size in sizes],
            out_shape=[f_shape(size) for size in sizes],
            scratch_shapes=[pltpu.VMEM((coefficients, pool_width), jnp.float32)],
            compiler_params=params,
            cost_estimate=cost,
        )(multipoles, operators, target, source)

    segments = [multipoles]
    for cut in range(cuts):
        def export_body(*refs, cut=cut):
            export_kernel(starts[: cut + 1], *refs)

        exported = call(
            export_body,
            jax.ShapeDtypeStruct((coefficients, sent), jnp.bfloat16),
            [boundary[cut : cut + 1]] + segments,
        )
        segments.append(from_partner(exported, axes, cuts - 1 - cut))

    def forward_body(*refs):
        forward_kernel(starts, *refs)

    with jax.named_scope("forward_terms"):
        local = pl.pallas_call(
            forward_body,
            grid=(steps,),
            in_specs=[whole(coefficients, size) for size in sizes]
            + [
                pl.BlockSpec((group, coefficients, coefficients), lambda i: (i, 0, 0)),
                row_spec,
                row_spec,
            ],
            out_specs=whole(coefficients, cells),
            out_shape=f_shape(cells),
            scratch_shapes=[pltpu.VMEM((coefficients, pool_width), jnp.bfloat16)],
            compiler_params=params,
            cost_estimate=cost,
        )(*segments, operators, target, source)

    returned = []
    for cut in reversed(range(cuts)):
        outgoing = expansions[cut + 1]
        if returned:
            def return_body(*refs, cut=cut):
                return_kernel(starts[cut + 1], 1, *refs)

            outgoing = call(return_body, f_shape(sent), [boundary, outgoing] + returned)
        returned.insert(0, from_partner(outgoing, axes, cuts - 1 - cut))

    def final_body(*refs):
        return_kernel(0, 2, *refs)

    return call(final_body, f_shape(cells), [boundary, expansions[0], local] + returned)


def solution(mesh):
    split = P(None, ("gx", "gy"))
    return jax.shard_map(
        per_device,
        mesh=mesh,
        in_specs=(split, P(), split, split, split, split),
        out_specs=split,
        check_vma=False,
    )
```

```python
import math

import jax
import jax.numpy as jnp
from jax import lax
from jax.experimental import pallas as pl
from jax.experimental.pallas import tpu as pltpu
from jax.sharding import PartitionSpec as P

LANES = 128
CHUNK = 512
ROWS = CHUNK // LANES
AXES = ("gx", "gy")
VMEM = pl.BlockSpec(memory_space=pltpu.VMEM)
SMEM = pl.BlockSpec(memory_space=pltpu.SMEM)
BF16 = jnp.bfloat16
F32 = jnp.float32


def up(size, multiple):
    return -(-size // multiple) * multiple


def params(mebibytes):
    return pltpu.CompilerParams(vmem_limit_bytes=mebibytes * 1024 * 1024)


def shape(rows, columns, kind):
    return jax.ShapeDtypeStruct((rows, columns), kind)


def call(kernel, out_shape, args, limit=4, scalars=0, scratch=(), flops=0):
    single = not isinstance(out_shape, (tuple, list))
    return pl.pallas_call(
        kernel,
        out_shape=out_shape,
        in_specs=[SMEM] * scalars + [VMEM] * (len(args) - scalars),
        out_specs=VMEM if single else [VMEM] * len(out_shape),
        scratch_shapes=list(scratch),
        compiler_params=params(limit),
        cost_estimate=pl.CostEstimate(flops=flops, bytes_accessed=1024, transcendentals=0),
    )(*args)


def dot(a, b):
    return jnp.dot(a, b, preferred_element_type=F32)


def dot_nt(a, b):
    return lax.dot_general(a, b, (((1,), (1,)), ((), ())), preferred_element_type=F32)


def halves(wide):
    high = wide.astype(BF16)
    return high, (wide - high.astype(F32)).astype(BF16)


def from_partner(block, distance):
    count = lax.axis_size(AXES)
    route = []
    for low in range(count):
        high = low | 1 << distance
        if high != low and high < count:
            route += [(low, high), (high, low)]
    return lax.ppermute(block, AXES, route)


def one_hot(row, first, height):
    place = lax.broadcasted_iota(jnp.int32, (height, row.shape[1]), 0)
    return jnp.where(place == row - first, 1.0, 0.0).astype(BF16)


def fill_hot(hot, index_ref, row, first, height):
    for n in range(ROWS):
        index = index_ref[pl.ds(row + n, 1), :]
        for low in range(0, height, LANES):
            size = min(LANES, height - low)
            hot[low : low + size, n * LANES : (n + 1) * LANES] = one_hot(index, first + low, size)


def total_of(count_ref):
    return lax.fori_loop(0, count_ref.shape[0], lambda i, t: t + count_ref[i], 0, unroll=8)


def pack_kernel(count_ref, target_ref, source_ref, packed_target, packed_source):
    classes, width = target_ref.shape
    lane = lax.broadcasted_iota(jnp.int32, (1, LANES), 1)

    def place(c, offset):
        shift = lax.rem(offset, LANES)
        row = offset // LANES
        keep = lane >= shift
        for ref, out in ((target_ref, packed_target), (source_ref, packed_source)):
            turned = pltpu.roll(ref[pl.ds(c, 1), :], shift, 1)
            out[pl.ds(row, 1), :] = jnp.where(keep, turned, out[pl.ds(row, 1), :])
            out[pl.ds(row + 1, 1), :] = turned
        return offset + count_ref[c]

    total = lax.fori_loop(0, classes, place, 0, unroll=8)
    position = lax.broadcasted_iota(jnp.int32, packed_target.shape, 0) * LANES
    position = position + lax.broadcasted_iota(jnp.int32, packed_target.shape, 1)
    for out in (packed_target, packed_source):
        out[...] = jnp.where(position < total, out[...], -1)


def order_kernel(coefficients, group, in_ref, out_ref):
    rows, classes, _ = in_ref.shape
    step = pl.program_id(0)
    tile = 16
    size = tile * group
    to = lax.broadcasted_iota(jnp.int32, (size, size), 0)
    of = lax.broadcasted_iota(jnp.int32, (size, size), 1)
    swap = (of == lax.rem(to, tile) * group + to // tile).astype(F32).astype(BF16)
    out_ref[...] = jnp.zeros_like(out_ref)
    row = lax.broadcasted_iota(jnp.int32, (size, coefficients), 0) // group
    for i in range(0, rows, tile):
        left = coefficients - step * rows - i
        for c in range(0, classes, group):
            block = in_ref[i : i + tile, c : c + group, :].reshape(size, coefficients)
            block = jnp.where(row < left, block, jnp.zeros_like(block))
            turned = dot(swap, block).astype(BF16)
            out_ref[c : c + group, i : i + tile, :coefficients] = turned.reshape(
                group, tile, coefficients
            )


def terms_kernel(starts, flip, count_ref, index_ref, op_ref, *refs):
    segs = refs[: len(starts)]
    out_ref, pool, hot, picked = refs[len(starts) :]
    classes, rows, depth = op_ref.shape
    height = pool.shape[1]
    total = total_of(count_ref)

    pool[...] = jnp.zeros_like(pool)
    for seg, first in zip(segs, starts):
        pool[: seg.shape[0], first : first + seg.shape[1]] = seg[...]
    picked[rows:, :] = jnp.zeros((depth - rows, picked.shape[1]), BF16)

    def pick(k, _):
        fill_hot(hot, index_ref, k * ROWS, 0, height)
        at = pl.ds(pl.multiple_of(k * CHUNK, CHUNK), CHUNK)
        picked[:rows, at] = dot(pool[...], hot[...]).astype(BF16)
        return 0

    lax.fori_loop(0, pl.cdiv(total, CHUNK), pick, 0)
    last = pl.multiple_of(total // CHUNK * CHUNK, CHUNK)
    out_ref[:, pl.ds(last, CHUNK)] = jnp.zeros((2 * rows, CHUNK), BF16)
    lane = lax.broadcasted_iota(jnp.int32, (rows, LANES), 1)

    def apply(c, offset):
        start = pl.multiple_of(offset // LANES * LANES, LANES)
        c_op = classes - 1 - c if flip else c
        new = dot(op_ref[c_op], picked[:, pl.ds(start, 2 * LANES)])
        keep = lane >= offset - start
        for first, part in zip((0, rows), halves(new)):
            at = pl.ds(start, LANES)
            old = out_ref[first : first + rows, at]
            out_ref[first : first + rows, at] = jnp.where(keep, part[:, :LANES], old)
            out_ref[first : first + rows, pl.ds(start + LANES, LANES)] = part[:, LANES:]
        return offset + count_ref[c]

    lax.fori_loop(0, classes, apply, 0, unroll=8)


def scatter_kernel(starts, count_ref, index_ref, terms_ref, *refs):
    outs = refs[: len(starts)]
    hot, sums = refs[len(starts) :]
    first, height = starts[0], hot.shape[0]
    total = total_of(count_ref)
    sums[...] = jnp.zeros_like(sums)

    def add(k, _):
        fill_hot(hot, index_ref, k * ROWS, first, height)
        at = pl.ds(pl.multiple_of(k * CHUNK, CHUNK), CHUNK)
        sums[...] += dot_nt(terms_ref[:, at], hot[...])
        return 0

    lax.fori_loop(0, pl.cdiv(total, CHUNK), add, 0)
    rows = sums.shape[0] // 2
    for out, start in zip(outs, starts):
        low = start - first
        at = slice(low, low + out.shape[1])
        out[...] = sums[: out.shape[0], at] + sums[rows : rows + out.shape[0], at]


def export_kernel(starts, cut, lists_ref, *refs):
    segs, out_ref = refs[:-1], refs[-1]
    row = lists_ref[cut : cut + 1, :]
    out = 0.0
    for seg, first in zip(segs, starts):
        out = out + dot(seg[...], one_hot(row, first, seg.shape[1]))
    out_ref[...] = out.astype(BF16)


def return_kernel(first, bases, lists_ref, *refs):
    out_ref = refs[-1]
    returned = refs[bases:-1]
    out = refs[0][...]
    for ref in refs[1:bases]:
        out = out + ref[...]
    cut = lists_ref.shape[0] - len(returned)
    for i, ref in enumerate(returned):
        hot = one_hot(lists_ref[cut + i : cut + i + 1, :], first, out_ref.shape[1])
        high, low = halves(ref[...])
        out = out + dot_nt(high, hot) + dot_nt(low, hot)
    out_ref[...] = out


def per_device(multipoles, operators, boundary, pair_target, pair_source, pair_count):
    coefficients, cells = multipoles.shape
    cuts, sent = boundary.shape
    classes, width = pair_target.shape
    starts = [0] + [cells + cut * sent for cut in range(cuts)]
    sizes = [cells] + [sent] * cuts
    pool_width = cells + cuts * sent
    rows, depth = up(coefficients, 16), up(coefficients, LANES)
    packed = classes * width + CHUNK
    counts = pair_count.reshape(classes)

    with jax.named_scope("pack_slots"):
        index_shape = shape(packed // LANES, LANES, jnp.int32)
        targets, sources = call(
            pack_kernel, [index_shape, index_shape], [counts, pair_target, pair_source], scalars=1
        )

    with jax.named_scope("order_operators"):
        group = math.gcd(classes, 16)
        block = 32
        ordered = pl.pallas_call(
            lambda *refs: order_kernel(coefficients, group, *refs),
            grid=(pl.cdiv(rows, block),),
            in_specs=[pl.BlockSpec((block, classes, coefficients), lambda i: (i, 0, 0))],
            out_specs=pl.BlockSpec((classes, block, depth), lambda i: (0, i, 0)),
            out_shape=jax.ShapeDtypeStruct((classes, rows, depth), BF16),
            compiler_params=params(16),
        )(operators.transpose(1, 0, 2))

    def terms(segments, index, flip):
        height = sum(segment.shape[1] for segment in segments)
        return call(
            lambda *refs: terms_kernel(starts[: len(segments)], flip, *refs),
            shape(2 * rows, packed, BF16),
            [counts, index, ordered] + list(segments),
            limit=16,
            scalars=1,
            scratch=[
                pltpu.VMEM((rows, height), BF16),
                pltpu.VMEM((height, CHUNK), BF16),
                pltpu.VMEM((depth, packed), BF16),
            ],
            flops=classes * width * rows * (height + depth),
        )

    def scatter(values, index, first, last):
        height = sum(sizes[first:last])
        return call(
            lambda *refs: scatter_kernel(starts[first:last], *refs),
            [shape(coefficients, size, F32) for size in sizes[first:last]],
            [counts, index, values],
            limit=8,
            scalars=1,
            scratch=[
                pltpu.VMEM((height, CHUNK), BF16),
                pltpu.VMEM((2 * rows, height), F32),
            ],
            flops=classes * width * rows * height * 2,
        )

    with jax.named_scope("reverse_terms"):
        back = terms([multipoles], targets, True)
        sums = [None] * (cuts + 1)
        last = cuts + 1
        while last > 0:
            first = max(last - 2, 0) if last > 2 else 0
            sums[first:last] = scatter(back, sources, first, last)
            last = first

    segments = [multipoles]
    for cut in range(cuts):
        with jax.named_scope("export"):
            exported = call(
                lambda *refs, cut=cut: export_kernel(starts, cut, *refs),
                shape(coefficients, sent, BF16),
                [boundary] + segments,
            )
        segments.append(from_partner(exported, cuts - 1 - cut))

    with jax.named_scope("forward_terms"):
        ahead = terms(segments, sources, False)
        (local,) = scatter(ahead, targets, 0, 1)

    returned = []
    for cut in reversed(range(cuts)):
        outgoing = sums[cut + 1]
        if returned:
            with jax.named_scope("return"):
                outgoing = call(
                    lambda *refs, cut=cut: return_kernel(starts[cut + 1], 1, *refs),
                    shape(coefficients, sent, F32),
                    [boundary, outgoing] + returned,
                )
        returned.insert(0, from_partner(outgoing, cuts - 1 - cut))

    with jax.named_scope("sum"):
        return call(
            lambda *refs: return_kernel(0, 2, *refs),
            shape(coefficients, cells, F32),
            [boundary, sums[0], local] + returned,
        )


def solution(mesh):
    split = P(None, AXES)
    return jax.shard_map(
        per_device,
        mesh=mesh,
        in_specs=(split, P(), split, split, split, split),
        out_specs=split,
        check_vma=False,
    )
```

```python
import math

import jax
import jax.numpy as jnp
from jax import lax
from jax.experimental import pallas as pl
from jax.experimental.pallas import tpu as pltpu
from jax.sharding import PartitionSpec as P

LANES = 128
CHUNK = 512
PICK_PART = 8
SCATTER_PART = 8
TILE = 16
AXES = ("gx", "gy")
VMEM = pl.BlockSpec(memory_space=pltpu.VMEM)
BF16 = jnp.bfloat16
F32 = jnp.float32


def up(size, multiple):
    return -(-size // multiple) * multiple


def params(mebibytes):
    return pltpu.CompilerParams(vmem_limit_bytes=mebibytes * 1024 * 1024)


def shape(rows, columns, kind):
    return jax.ShapeDtypeStruct((rows, columns), kind)


def call(kernel, out_shape, args, after, limit=4, scratch=(), us=0.3):
    single = not isinstance(out_shape, (tuple, list))
    return pl.pallas_call(
        lambda _, *refs: kernel(*refs),
        out_shape=out_shape,
        in_specs=[pl.BlockSpec(memory_space=pl.ANY)] + [VMEM] * len(args),
        out_specs=VMEM if single else [VMEM] * len(out_shape),
        scratch_shapes=list(scratch),
        compiler_params=params(limit),
        cost_estimate=takes(us),
    )(after, *args)


def takes(us):
    return pl.CostEstimate(flops=int(us * 1e9), bytes_accessed=0, transcendentals=0)


def dot(a, b):
    return jnp.dot(a, b, preferred_element_type=F32)


def dot_nt(a, b):
    return lax.dot_general(a, b, (((1,), (1,)), ((), ())), preferred_element_type=F32)


def halves(wide):
    high = wide.astype(BF16)
    return high, (wide - high.astype(F32)).astype(BF16)


def from_partner(block, distance):
    count = lax.axis_size(AXES)
    route = []
    for low in range(count):
        high = low | 1 << distance
        if high != low and high < count:
            route += [(low, high), (high, low)]
    return lax.ppermute(block, AXES, route)


def one_hot(row, first, height):
    place = lax.broadcasted_iota(jnp.int32, (height, row.shape[1]), 0)
    return jnp.where(place == row - first, 1.0, 0.0).astype(BF16)


def hot_columns(index_ref, row, count, first, height):
    columns = []
    for n in range(count):
        index = index_ref[pl.ds(row + n, 1), :]
        blocks = [
            one_hot(index, first + low, min(LANES, height - low))
            for low in range(0, height, LANES)
        ]
        columns.append(jnp.concatenate(blocks, axis=0))
    return jnp.concatenate(columns, axis=1)


def for_parts(total, largest, body):
    chunks = pl.cdiv(total, CHUNK)
    chunks = jnp.where(lax.rem(chunks, 4) == 3, chunks + 1, chunks)

    def whole(k, _):
        body(k * largest, largest)
        return 0

    lax.fori_loop(0, chunks // largest, whole, 0)
    size = largest // 2
    while size:
        done = chunks // (2 * size) * (2 * size)

        @pl.when(lax.rem(chunks // size, 2) == 1)
        def _(done=done, size=size):
            body(done, size)

        size //= 2


def pick_columns(total, index_ref, pool, picked):
    def pick(first, size):
        lanes = size * CHUNK
        row = first * (CHUNK // LANES)
        hot = hot_columns(index_ref, row, lanes // LANES, 0, pool.shape[1])
        at = pl.ds(pl.multiple_of(first * CHUNK, CHUNK), lanes)
        picked[:, at] = dot(pool[...], hot).astype(BF16)

    for_parts(total, PICK_PART, pick)


def pack_kernel(
    classes, meta_ref, mult_ref, packed_target, packed_source, info_ref, picked, pool
):
    lane = lax.broadcasted_iota(jnp.int32, (1, LANES), 1)

    def place(c, offset):
        info_ref[pl.ds(c, 1), :] = jnp.full((1, LANES), offset, jnp.int32)
        shift = lax.rem(offset, LANES)
        row = offset // LANES
        keep = lane >= shift
        for first, out in ((0, packed_target), (classes, packed_source)):
            turned = pltpu.roll(meta_ref[pl.ds(first + c, 1), :], shift, 1)
            out[pl.ds(row, 1), :] = jnp.where(keep, turned, out[pl.ds(row, 1), :])
            out[pl.ds(row + 1, 1), :] = turned
        return offset + meta_ref[2 * classes + c, 0]

    total = lax.fori_loop(0, classes, place, 0, unroll=8)
    info_ref[classes:, :] = jnp.full((8, LANES), total, jnp.int32)
    position = lax.broadcasted_iota(jnp.int32, packed_target.shape, 0) * LANES
    position = position + lax.broadcasted_iota(jnp.int32, packed_target.shape, 1)
    for out in (packed_target, packed_source):
        out[...] = jnp.where(position < total, out[...], -1)

    pool[...] = jnp.zeros_like(pool)
    pool[: mult_ref.shape[0], :] = mult_ref[...]
    pick_columns(total, packed_target, pool, picked)


def order_kernel(op_ref, ordered):
    for i in range(0, op_ref.shape[0], TILE):
        size = min(TILE, op_ref.shape[0] - i)
        block = jnp.swapaxes(op_ref[i : i + size], 0, 1)
        ordered[:, i : i + size, :] = block


def pick_kernel(starts, info_ref, index_ref, *refs):
    segs = refs[: len(starts)]
    picked, pool = refs[len(starts) :]
    pool[...] = jnp.zeros_like(pool)
    for seg, first in zip(segs, starts):
        pool[: seg.shape[0], first : first + seg.shape[1]] = seg[...]
    pick_columns(info_ref[info_ref.shape[0] - 1, 0], index_ref, pool, picked)


def apply_kernel(flip, info_ref, op_ref, picked, out_ref):
    classes, rows, depth = op_ref.shape
    last = pl.multiple_of(info_ref[classes, 0] // CHUNK * CHUNK, CHUNK)
    out_ref[:, pl.ds(last, 2 * CHUNK)] = jnp.zeros((2 * rows, 2 * CHUNK), BF16)
    lane = lax.broadcasted_iota(jnp.int32, (rows, LANES), 1)

    def apply(c, _):
        offset = info_ref[c, 0]
        start = pl.multiple_of(offset // LANES * LANES, LANES)
        c_op = classes - 1 - c if flip else c
        new = dot(op_ref[c_op], picked[:depth, pl.ds(start, 2 * LANES)])
        keep = lane >= offset - start
        for first, part in zip((0, rows), halves(new)):
            at = pl.ds(start, LANES)
            old = out_ref[first : first + rows, at]
            out_ref[first : first + rows, at] = jnp.where(keep, part[:, :LANES], old)
            out_ref[first : first + rows, pl.ds(start + LANES, LANES)] = part[:, LANES:]
        return 0

    lax.fori_loop(0, classes, apply, 0, unroll=16)


def add_terms(first, info_ref, index_ref, terms_ref, sums):
    def add(part, size):
        lanes = size * CHUNK
        row = part * (CHUNK // LANES)
        hot = hot_columns(index_ref, row, lanes // LANES, first, sums.shape[1])
        at = pl.ds(pl.multiple_of(part * CHUNK, CHUNK), lanes)
        sums[...] += dot_nt(terms_ref[:, at], hot)

    for_parts(info_ref[info_ref.shape[0] - 1, 0], SCATTER_PART, add)


def scatter_kernel(starts, info_ref, index_ref, terms_ref, *refs):
    outs, sums = refs[:-1], refs[-1]
    sums[...] = jnp.zeros_like(sums)
    add_terms(starts[0], info_ref, index_ref, terms_ref, sums)
    rows = sums.shape[0] // 2
    for out, start in zip(outs, starts):
        low = start - starts[0]
        at = slice(low, low + out.shape[1])
        out[...] = sums[: out.shape[0], at] + sums[rows : rows + out.shape[0], at]


def export_kernel(starts, list_row, meta_ref, *refs):
    segs, out_ref = refs[: len(starts)], refs[len(starts)]
    row = meta_ref[list_row : list_row + 1, :]
    out = 0.0
    for seg, first in zip(segs, starts):
        out = out + dot(seg[...], one_hot(row, first, seg.shape[1]))
    out_ref[...] = out.astype(BF16)
    for own in refs[len(starts) + 1 :]:
        own[...] = segs[0][...]


def came_back(first, row, meta_ref, returned, width):
    out = 0.0
    for i, ref in enumerate(returned):
        hot = one_hot(meta_ref[row + i : row + i + 1, :], first, width)
        high, low = halves(ref[...])
        out = out + dot_nt(high, hot) + dot_nt(low, hot)
    return out


def return_kernel(first, row, meta_ref, base_ref, *refs):
    returned, out_ref = refs[:-1], refs[-1]
    out_ref[...] = base_ref[...] + came_back(first, row, meta_ref, returned, out_ref.shape[1])


def local_kernel(
    row, meta_ref, info_ref, target_ref, ahead_ref, source_ref, back_ref, *refs
):
    returned, (out_ref, sums) = refs[:-2], refs[-2:]
    count, rows = out_ref.shape[0], sums.shape[0] // 2
    sums[...] = jnp.zeros_like(sums)
    add_terms(0, info_ref, target_ref, ahead_ref, sums)
    add_terms(0, info_ref, source_ref, back_ref, sums)
    out = came_back(0, row, meta_ref, returned, out_ref.shape[1])
    out_ref[...] = out + (sums[:count, :] + sums[rows : rows + count, :])


def per_device(multipoles, operators, boundary, pair_target, pair_source, pair_count):
    coefficients, cells = multipoles.shape
    cuts, sent = boundary.shape
    classes, width = pair_target.shape
    starts = [0] + [cells + cut * sent for cut in range(cuts)]
    sizes = [cells] + [sent] * cuts
    pool_width = cells + cuts * sent
    rows = up(coefficients, TILE)
    packed = classes * width + 2 * CHUNK + LANES

    index_shape = shape(packed // LANES, LANES, jnp.int32)

    def pick(segments, index, after):
        height = sum(segment.shape[1] for segment in segments)
        return call(
            lambda *refs: pick_kernel(starts, *refs),
            shape(rows, packed, BF16),
            [info, index] + list(segments),
            after,
            limit=16,
            scratch=[pltpu.VMEM((rows, height), BF16)],
            us=2.0,
        )

    def apply(columns, flip, after):
        return call(
            lambda *refs: apply_kernel(flip, *refs),
            shape(2 * rows, packed, BF16),
            [info, ordered, columns],
            after,
            limit=8,
            us=5.0,
        )

    def scatter(values, index, first, last, after):
        height = sum(sizes[first:last])
        return call(
            lambda *refs: scatter_kernel(starts[first:last], *refs),
            [shape(coefficients, size, F32) for size in sizes[first:last]],
            [info, index, values],
            after,
            limit=8,
            scratch=[pltpu.VMEM((2 * rows, height), F32)],
            us=1.0,
        )

    segments, returned, sums = [multipoles], [], [None] * (cuts + 1)
    meta = jnp.concatenate(
        [pair_target, pair_source, jnp.broadcast_to(pair_count, pair_target.shape), boundary], axis=0
    )

    def export(after):
        cut = len(segments) - 1
        with jax.named_scope("export"):
            out = [shape(coefficients, sent, BF16)]
            if cut == 0:
                out.append(shape(coefficients, cells, BF16))
            exported, *own = call(
                lambda *refs: export_kernel(starts[: cut + 1], 3 * classes + cut, *refs),
                out,
                [meta] + segments,
                after,
            )
            segments[:1] = own or segments[:1]
        segments.append(from_partner(exported, cuts - 1 - cut))
        return exported

    def give_back(after):
        cut = cuts - 1 - len(returned)
        outgoing = sums[cut + 1]
        if returned:
            with jax.named_scope("return"):
                outgoing = call(
                    lambda *refs: return_kernel(starts[cut + 1], 3 * classes + cut + 1, *refs),
                    shape(coefficients, sent, F32),
                    [meta, outgoing] + returned,
                    after,
                )
        returned.insert(0, from_partner(outgoing, cuts - 1 - cut))
        return outgoing

    def more_sums(after):
        last = max((cut for cut in range(1, cuts + 1) if sums[cut] is None), default=0)
        if last == 0:
            return after
        first = max(last - 1, 1)
        with jax.named_scope("reverse_sums"):
            sums[first : last + 1] = scatter(back, sources, first, last + 1, after)
        return sums[first]

    step = export(meta)
    with jax.named_scope("pack_slots"):
        targets, sources, info, picked = pl.pallas_call(
            lambda _, *refs: pack_kernel(classes, *refs),
            out_shape=[
                index_shape,
                index_shape,
                shape(classes + 8, LANES, jnp.int32),
                shape(rows, packed, BF16),
            ],
            in_specs=[pl.BlockSpec(memory_space=pl.ANY), VMEM, VMEM],
            out_specs=[VMEM] * 4,
            scratch_shapes=[pltpu.VMEM((rows, cells), BF16)],
            compiler_params=params(8),
            cost_estimate=takes(2.5),
        )(step, meta, segments[0])
    step = export(info)
    with jax.named_scope("order_operators"):
        ordered = call(
            order_kernel,
            jax.ShapeDtypeStruct((classes, rows, coefficients), BF16),
            [operators.transpose(1, 0, 2)],
            step,
            limit=8,
            us=1.3,
        )
    step = export(ordered)
    with jax.named_scope("reverse_terms"):
        back = apply(picked, True, step)
    step = export(back)
    step = more_sums(step)
    step = give_back(step)
    while len(segments) <= cuts:
        step = export(step)
    step = more_sums(step)
    step = give_back(step)
    with jax.named_scope("forward_columns"):
        ahead = pick(segments, sources, step)
    step = give_back(ahead)
    with jax.named_scope("forward_terms"):
        ahead = apply(ahead, False, step)
    step = ahead
    while len(returned) < cuts:
        step = give_back(step)
        step = more_sums(step)
    with jax.named_scope("local_sums"):
        local = call(
            lambda *refs: local_kernel(3 * classes + 1, *refs),
            shape(coefficients, cells, F32),
            [meta, info, targets, ahead, sources, back] + returned[1:],
            step,
            limit=8,
            scratch=[pltpu.VMEM((2 * rows, cells), F32)],
            us=2.0,
        )
    with jax.named_scope("last_sum"):
        return call(
            lambda *refs: return_kernel(0, 3 * classes, *refs),
            shape(coefficients, cells, F32),
            [meta, local, returned[0]],
            local,
        )


def solution(mesh):
    split = P(None, AXES)
    return jax.shard_map(
        per_device,
        mesh=mesh,
        in_specs=(split, P(), split, split, split, split),
        out_specs=split,
        check_vma=False,
    )
```

```python
import math

import jax
import jax.numpy as jnp
from jax import lax
from jax.experimental import pallas as pl
from jax.experimental.pallas import tpu as pltpu
from jax.sharding import PartitionSpec as P

LANES = 128
CHUNK = 512
PICK_PART = 8
UNROLL = 16
SCATTER_PART = 8
TILE = 16
AXES = ("gx", "gy")
VMEM = pl.BlockSpec(memory_space=pltpu.VMEM)
BF16 = jnp.bfloat16
F32 = jnp.float32


def up(size, multiple):
    return -(-size // multiple) * multiple


def params(mebibytes):
    return pltpu.CompilerParams(vmem_limit_bytes=mebibytes * 1024 * 1024)


def shape(rows, columns, kind):
    return jax.ShapeDtypeStruct((rows, columns), kind)


def call(kernel, out_shape, args, after, limit=4, scratch=(), us=0.3, **more):
    single = not isinstance(out_shape, (tuple, list))
    return pl.pallas_call(
        lambda _, *refs: kernel(*refs),
        out_shape=out_shape,
        in_specs=[pl.BlockSpec(memory_space=pl.ANY)] + [VMEM] * len(args),
        out_specs=VMEM if single else [VMEM] * len(out_shape),
        scratch_shapes=list(scratch),
        compiler_params=params(limit),
        cost_estimate=takes(us),
        **more,
    )(after, *args)


def takes(us):
    return pl.CostEstimate(flops=int(us * 1e9), bytes_accessed=0, transcendentals=0)


def dot(a, b):
    return jnp.dot(a, b, preferred_element_type=F32)


def dot_nt(a, b):
    return lax.dot_general(a, b, (((1,), (1,)), ((), ())), preferred_element_type=F32)


def halves(wide):
    high = wide.astype(BF16)
    return high, (wide - high.astype(F32)).astype(BF16)


def from_partner(block, distance):
    count = lax.axis_size(AXES)
    route = []
    for low in range(count):
        high = low | 1 << distance
        if high != low and high < count:
            route += [(low, high), (high, low)]
    return lax.ppermute(block, AXES, route)


def one_hot(row, first, height):
    place = lax.broadcasted_iota(jnp.int32, (height, row.shape[1]), 0)
    return jnp.where(place == row - first, 1.0, 0.0).astype(BF16)


def hot_columns(index_ref, row, count, first, height):
    columns = []
    for n in range(count):
        index = index_ref[pl.ds(row + n, 1), :]
        blocks = [
            one_hot(index, first + low, min(LANES, height - low))
            for low in range(0, height, LANES)
        ]
        columns.append(jnp.concatenate(blocks, axis=0))
    return jnp.concatenate(columns, axis=1)


def for_parts(total, largest, body):
    chunks = pl.cdiv(total, CHUNK)
    chunks = jnp.where(lax.rem(chunks, 4) == 3, chunks + 1, chunks)

    def whole(k, _):
        body(k * largest, largest)
        return 0

    lax.fori_loop(0, chunks // largest, whole, 0)
    size = largest // 2
    while size:
        done = chunks // (2 * size) * (2 * size)

        @pl.when(lax.rem(chunks // size, 2) == 1)
        def _(done=done, size=size):
            body(done, size)

        size //= 2


def pick_columns(total, index_ref, pool, picked):
    def pick(first, size):
        lanes = size * CHUNK
        row = first * (CHUNK // LANES)
        hot = hot_columns(index_ref, row, lanes // LANES, 0, pool.shape[1])
        at = pl.ds(pl.multiple_of(first * CHUNK, CHUNK), lanes)
        picked[:, at] = dot(pool[...], hot).astype(BF16)

    for_parts(total, PICK_PART, pick)


def pack_kernel(
    classes, meta_ref, mult_ref, packed_target, packed_source, info_ref, picked, pool
):
    lane = lax.broadcasted_iota(jnp.int32, (1, LANES), 1)

    def place(c, offset):
        info_ref[pl.ds(c, 1), :] = jnp.full((1, LANES), offset, jnp.int32)
        shift = lax.rem(offset, LANES)
        row = offset // LANES
        keep = lane >= shift
        for first, out in ((0, packed_target), (classes, packed_source)):
            turned = pltpu.roll(meta_ref[pl.ds(first + c, 1), :], shift, 1)
            out[pl.ds(row, 1), :] = jnp.where(keep, turned, out[pl.ds(row, 1), :])
            out[pl.ds(row + 1, 1), :] = turned
        return offset + meta_ref[2 * classes + c, 0]

    total = lax.fori_loop(0, classes, place, 0, unroll=8)
    info_ref[classes:, :] = jnp.full((8, LANES), total, jnp.int32)
    position = lax.broadcasted_iota(jnp.int32, packed_target.shape, 0) * LANES
    position = position + lax.broadcasted_iota(jnp.int32, packed_target.shape, 1)
    for out in (packed_target, packed_source):
        out[...] = jnp.where(position < total, out[...], -1)

    pool[...] = jnp.zeros_like(pool)
    pool[: mult_ref.shape[0], :] = mult_ref[...]
    pick_columns(total, packed_target, pool, picked)


def order_kernel(op_ref, ordered):
    for i in range(0, op_ref.shape[0], TILE):
        size = min(TILE, op_ref.shape[0] - i)
        block = jnp.swapaxes(op_ref[i : i + size], 0, 1)
        ordered[:, i : i + size, :] = block


def pick_kernel(starts, info_ref, index_ref, *refs):
    segs = refs[: len(starts)]
    picked, pool = refs[len(starts) :]
    pool[...] = jnp.zeros_like(pool)
    for seg, first in zip(segs, starts):
        pool[: seg.shape[0], first : first + seg.shape[1]] = seg[...]
    pick_columns(info_ref[info_ref.shape[0] - 1, 0], index_ref, pool, picked)


def apply_kernel(flip, first_class, last_class, info_ref, op_ref, picked, *refs):
    out_ref = refs[-1]
    classes, rows, depth = op_ref.shape
    if first_class == 0:
        last = pl.multiple_of(info_ref[classes, 0] // CHUNK * CHUNK, CHUNK)
        out_ref[:, pl.ds(last, 2 * CHUNK)] = jnp.zeros((2 * rows, 2 * CHUNK), BF16)
    lane = lax.broadcasted_iota(jnp.int32, (rows, LANES), 1)

    def apply(c, _):
        offset = info_ref[c, 0]
        start = pl.multiple_of(offset // LANES * LANES, LANES)
        c_op = classes - 1 - c if flip else c
        new = dot(op_ref[c_op], picked[:depth, pl.ds(start, 2 * LANES)])
        keep = lane >= offset - start
        for first, part in zip((0, rows), halves(new)):
            at = pl.ds(start, LANES)
            old = out_ref[first : first + rows, at]
            out_ref[first : first + rows, at] = jnp.where(keep, part[:, :LANES], old)
            out_ref[first : first + rows, pl.ds(start + LANES, LANES)] = part[:, LANES:]
        return 0

    lax.fori_loop(first_class, last_class, apply, 0, unroll=UNROLL)


def add_terms(first, info_ref, index_ref, terms_ref, sums):
    def add(part, size):
        lanes = size * CHUNK
        row = part * (CHUNK // LANES)
        hot = hot_columns(index_ref, row, lanes // LANES, first, sums.shape[1])
        at = pl.ds(pl.multiple_of(part * CHUNK, CHUNK), lanes)
        sums[...] += dot_nt(terms_ref[:, at], hot)

    for_parts(info_ref[info_ref.shape[0] - 1, 0], SCATTER_PART, add)


def scatter_kernel(starts, info_ref, index_ref, terms_ref, *refs):
    outs, sums = refs[:-1], refs[-1]
    sums[...] = jnp.zeros_like(sums)
    add_terms(starts[0], info_ref, index_ref, terms_ref, sums)
    rows = sums.shape[0] // 2
    for out, start in zip(outs, starts):
        low = start - starts[0]
        at = slice(low, low + out.shape[1])
        out[...] = sums[: out.shape[0], at] + sums[rows : rows + out.shape[0], at]


def export_kernel(starts, list_row, meta_ref, *refs):
    segs, out_ref = refs[: len(starts)], refs[len(starts)]
    row = meta_ref[list_row : list_row + 1, :]
    out = 0.0
    for seg, first in zip(segs, starts):
        out = out + dot(seg[...], one_hot(row, first, seg.shape[1]))
    out_ref[...] = out.astype(BF16)
    for own in refs[len(starts) + 1 :]:
        own[...] = segs[0][...]


def came_back(first, row, meta_ref, returned, width):
    out = 0.0
    for i, ref in enumerate(returned):
        hot = one_hot(meta_ref[row + i : row + i + 1, :], first, width)
        high, low = halves(ref[...])
        out = out + dot_nt(high, hot) + dot_nt(low, hot)
    return out


def return_kernel(first, row, meta_ref, base_ref, *refs):
    returned, out_ref = refs[:-1], refs[-1]
    out_ref[...] = base_ref[...] + came_back(first, row, meta_ref, returned, out_ref.shape[1])


def local_kernel(
    row, meta_ref, info_ref, target_ref, ahead_ref, source_ref, back_ref, *refs
):
    returned, (out_ref, sums) = refs[:-2], refs[-2:]
    count, rows = out_ref.shape[0], sums.shape[0] // 2
    sums[...] = jnp.zeros_like(sums)
    add_terms(0, info_ref, target_ref, ahead_ref, sums)
    add_terms(0, info_ref, source_ref, back_ref, sums)
    out = came_back(0, row, meta_ref, returned, out_ref.shape[1])
    out_ref[...] = out + (sums[:count, :] + sums[rows : rows + count, :])


def per_device(multipoles, operators, boundary, pair_target, pair_source, pair_count):
    coefficients, cells = multipoles.shape
    cuts, sent = boundary.shape
    classes, width = pair_target.shape
    starts = [0] + [cells + cut * sent for cut in range(cuts)]
    sizes = [cells] + [sent] * cuts
    pool_width = cells + cuts * sent
    rows = up(coefficients, TILE)
    packed = classes * width + 2 * CHUNK + LANES

    index_shape = shape(packed // LANES, LANES, jnp.int32)

    def pick(segments, index, after):
        height = sum(segment.shape[1] for segment in segments)
        return call(
            lambda *refs: pick_kernel(starts, *refs),
            shape(rows, packed, BF16),
            [info, index] + list(segments),
            after,
            limit=16,
            scratch=[pltpu.VMEM((rows, height), BF16)],
            us=4.0,
        )

    def apply(columns, flip, after, first, last, terms=()):
        return call(
            lambda *refs: apply_kernel(flip, first, last, *refs),
            shape(2 * rows, packed, BF16),
            [info, ordered, columns, *terms],
            after,
            limit=8,
            us=0.1,
            input_output_aliases={4: 0} if terms else {},
        )

    def scatter(values, index, first, last, after, us):
        height = sum(sizes[first:last])
        return call(
            lambda *refs: scatter_kernel(starts[first:last], *refs),
            [shape(coefficients, size, F32) for size in sizes[first:last]],
            [info, index, values],
            after,
            limit=8,
            scratch=[pltpu.VMEM((2 * rows, height), F32)],
            us=us,
        )

    segments, returned, sums = [multipoles], [], [None] * (cuts + 1)
    meta = jnp.concatenate(
        [pair_target, pair_source, jnp.broadcast_to(pair_count, pair_target.shape), boundary], axis=0
    )

    def export(after):
        cut = len(segments) - 1
        with jax.named_scope("export"):
            out = [shape(coefficients, sent, BF16)]
            if cut == 0:
                out.append(shape(coefficients, cells, BF16))
            exported, *own = call(
                lambda *refs: export_kernel(starts[: cut + 1], 3 * classes + cut, *refs),
                out,
                [meta] + segments,
                after,
            )
            segments[:1] = own or segments[:1]
        segments.append(from_partner(exported, cuts - 1 - cut))
        return exported

    def give_back(after):
        cut = cuts - 1 - len(returned)
        outgoing = sums[cut + 1]
        if returned:
            with jax.named_scope("return"):
                outgoing = call(
                    lambda *refs: return_kernel(starts[cut + 1], 3 * classes + cut + 1, *refs),
                    shape(coefficients, sent, F32),
                    [meta, outgoing] + returned,
                    after,
                )
        returned.insert(0, from_partner(outgoing, cuts - 1 - cut))
        return outgoing

    def more_sums(after, us):
        last = max((cut for cut in range(1, cuts + 1) if sums[cut] is None), default=0)
        if last == 0:
            return after
        first = max(last - 1, 1)
        with jax.named_scope("reverse_sums"):
            sums[first : last + 1] = scatter(back, sources, first, last + 1, after, us)
        return sums[first]

    step = export(meta)
    with jax.named_scope("pack_slots"):
        targets, sources, info, picked = pl.pallas_call(
            lambda _, *refs: pack_kernel(classes, *refs),
            out_shape=[
                index_shape,
                index_shape,
                shape(classes + 8, LANES, jnp.int32),
                shape(rows, packed, BF16),
            ],
            in_specs=[pl.BlockSpec(memory_space=pl.ANY), VMEM, VMEM],
            out_specs=[VMEM] * 4,
            scratch_shapes=[pltpu.VMEM((rows, cells), BF16)],
            compiler_params=params(8),
            cost_estimate=takes(2.5),
        )(step, meta, segments[0])
    with jax.named_scope("order_operators"):
        ordered = call(
            order_kernel,
            jax.ShapeDtypeStruct((classes, rows, coefficients), BF16),
            [operators.transpose(1, 0, 2)],
            info,
            limit=8,
            us=1.3,
        )
    early = min(16, classes // 2)
    step = export(ordered)
    with jax.named_scope("reverse_terms"):
        back = apply(picked, True, step, 0, early)
    step = export(back) if len(segments) <= cuts else back
    with jax.named_scope("reverse_terms"):
        back = apply(picked, True, step, early, classes, [back])
    step = more_sums(back, 0.1)
    step = give_back(step)
    step = export(step) if len(segments) <= cuts else step
    step = more_sums(step, 4.0)
    step = give_back(step)
    while len(segments) <= cuts:
        step = export(step)
    while any(part is None for part in sums[1:]):
        step = more_sums(step, 4.0)
    step = give_back(step)
    with jax.named_scope("forward_columns"):
        columns = pick(segments, sources, step)
    ends = [classes * part // 4 for part in range(5)]
    ahead, step = [], columns
    for part in range(4):
        after = columns
        if part >= 2 and len(returned) < cuts:
            after = give_back(ahead[0])
        with jax.named_scope("forward_terms"):
            ahead = [apply(columns, False, after, ends[part], ends[part + 1], ahead)]
    (ahead,) = ahead
    step = ahead
    while len(returned) < cuts:
        step = give_back(step)
    with jax.named_scope("local_sums"):
        local = call(
            lambda *refs: local_kernel(3 * classes + 1, *refs),
            shape(coefficients, cells, F32),
            [meta, info, targets, ahead, sources, back] + returned[1:],
            step,
            limit=8,
            scratch=[pltpu.VMEM((2 * rows, cells), F32)],
            us=0.1,
        )
    with jax.named_scope("last_sum"):
        return call(
            lambda *refs: return_kernel(0, 3 * classes, *refs),
            shape(coefficients, cells, F32),
            [meta, local, returned[0]],
            local,
        )


def solution(mesh):
    split = P(None, AXES)
    return jax.shard_map(
        per_device,
        mesh=mesh,
        in_specs=(split, P(), split, split, split, split),
        out_specs=split,
        check_vma=False,
    )
```

```python
import math

import jax
import jax.numpy as jnp
from jax import lax
from jax.experimental import pallas as pl
from jax.experimental.pallas import tpu as pltpu
from jax.sharding import PartitionSpec as P

LANES = 128
CHUNK = 512
PICK_PART = 8
UNROLL = 16
SCATTER_PART = 8
TILE = 16
AXES = ("gx", "gy")
VMEM = pl.BlockSpec(memory_space=pltpu.VMEM)
BF16 = jnp.bfloat16
F32 = jnp.float32


def up(size, multiple):
    return -(-size // multiple) * multiple


def params(mebibytes):
    return pltpu.CompilerParams(vmem_limit_bytes=mebibytes * 1024 * 1024)


def shape(rows, columns, kind):
    return jax.ShapeDtypeStruct((rows, columns), kind)


def call(kernel, out_shape, args, after, limit=4, scratch=(), us=0.3, **more):
    single = not isinstance(out_shape, (tuple, list))
    return pl.pallas_call(
        lambda _, *refs: kernel(*refs),
        out_shape=out_shape,
        in_specs=[pl.BlockSpec(memory_space=pl.ANY)] + [VMEM] * len(args),
        out_specs=VMEM if single else [VMEM] * len(out_shape),
        scratch_shapes=list(scratch),
        compiler_params=params(limit),
        cost_estimate=takes(us),
        **more,
    )(after, *args)


def takes(us):
    return pl.CostEstimate(flops=int(us * 1e9), bytes_accessed=0, transcendentals=0)


def dot(a, b):
    return jnp.dot(a, b, preferred_element_type=F32)


def dot_nt(a, b):
    return lax.dot_general(a, b, (((1,), (1,)), ((), ())), preferred_element_type=F32)


def halves(wide):
    high = wide.astype(BF16)
    return high, (wide - high.astype(F32)).astype(BF16)


def from_partner(block, distance):
    count = lax.axis_size(AXES)
    route = []
    for low in range(count):
        high = low | 1 << distance
        if high != low and high < count:
            route += [(low, high), (high, low)]
    return lax.ppermute(block, AXES, route)


def one_hot(row, first, height):
    place = lax.broadcasted_iota(jnp.int32, (height, row.shape[1]), 0)
    return jnp.where(place == row - first, 1.0, 0.0).astype(BF16)


def hot_columns(index_ref, row, count, first, height):
    columns = []
    for n in range(count):
        index = index_ref[pl.ds(row + n, 1), :]
        blocks = [
            one_hot(index, first + low, min(LANES, height - low))
            for low in range(0, height, LANES)
        ]
        columns.append(jnp.concatenate(blocks, axis=0))
    return jnp.concatenate(columns, axis=1)


def for_parts(total, largest, body):
    chunks = pl.cdiv(total, CHUNK)
    chunks = jnp.where(lax.rem(chunks, 4) == 3, chunks + 1, chunks)

    def whole(k, _):
        body(k * largest, largest)
        return 0

    lax.fori_loop(0, chunks // largest, whole, 0)
    size = largest // 2
    while size:
        done = chunks // (2 * size) * (2 * size)

        @pl.when(lax.rem(chunks // size, 2) == 1)
        def _(done=done, size=size):
            body(done, size)

        size //= 2


def pick_columns(total, index_ref, pool, picked):
    def pick(first, size):
        lanes = size * CHUNK
        row = first * (CHUNK // LANES)
        hot = hot_columns(index_ref, row, lanes // LANES, 0, pool.shape[1])
        at = pl.ds(pl.multiple_of(first * CHUNK, CHUNK), lanes)
        picked[:, at] = dot(pool[...], hot).astype(BF16)

    for_parts(total, PICK_PART, pick)


def pack_kernel(
    classes, shifts, meta_ref, mult_ref, packed_target, packed_source, info_ref, picked, pool, counts, codes
):
    to_source, to_count = shifts
    codes[...] = meta_ref[:, :LANES]
    slots = jnp.where(codes[...] >= 0, 1, 0)
    counts[...] = jnp.broadcast_to(jnp.sum(slots, axis=1, keepdims=True), slots.shape)
    lane = lax.broadcasted_iota(jnp.int32, (1, LANES), 1)

    def place(c, carry):
        offset, current = carry
        following = offset + counts[c, 0]
        info_ref[pl.ds(c, 1), :] = jnp.full((1, LANES), offset, jnp.int32)
        shift = lax.rem(offset, LANES)
        row = offset // LANES
        turned = pltpu.roll(codes[pl.ds(c, 1), :], shift, 1)
        current = jnp.where(lane >= shift, turned, current)
        packed_target[pl.ds(row, 1), :] = current
        packed_target[pl.ds(row + 1, 1), :] = turned
        return following, jnp.where(following // LANES == row, current, turned)

    none = jnp.zeros((1, LANES), jnp.int32)
    total, _ = lax.fori_loop(0, classes, place, (0, none), unroll=8)
    info_ref[classes:, :] = jnp.full((8, LANES), total, jnp.int32)
    position = lax.broadcasted_iota(jnp.int32, packed_target.shape, 0) * LANES
    position = position + lax.broadcasted_iota(jnp.int32, packed_target.shape, 1)
    used = position < total
    code = packed_target[...]
    source = (code >> to_source) & ((1 << (to_count - to_source)) - 1)
    packed_source[...] = jnp.where(used, source, -1)
    packed_target[...] = jnp.where(used, code & ((1 << to_source) - 1), -1)

    pool[...] = jnp.zeros_like(pool)
    pool[: mult_ref.shape[0], :] = mult_ref[...]
    pick_columns(total, packed_target, pool, picked)


def order_kernel(op_ref, ordered):
    for i in range(0, op_ref.shape[0], TILE):
        size = min(TILE, op_ref.shape[0] - i)
        block = jnp.swapaxes(op_ref[i : i + size], 0, 1)
        ordered[:, i : i + size, :] = block


def pick_kernel(starts, info_ref, index_ref, *refs):
    segs = refs[: len(starts)]
    picked, pool = refs[len(starts) :]
    pool[...] = jnp.zeros_like(pool)
    for seg, first in zip(segs, starts):
        pool[: seg.shape[0], first : first + seg.shape[1]] = seg[...]
    pick_columns(info_ref[info_ref.shape[0] - 1, 0], index_ref, pool, picked)


def apply_kernel(flip, first_class, last_class, info_ref, op_ref, picked, *refs):
    out_ref = refs[-1]
    classes, rows, depth = op_ref.shape
    if first_class == 0:
        last = pl.multiple_of(info_ref[classes, 0] // CHUNK * CHUNK, CHUNK)
        out_ref[:, pl.ds(last, 2 * CHUNK)] = jnp.zeros((2 * rows, 2 * CHUNK), BF16)
    lane = lax.broadcasted_iota(jnp.int32, (rows, LANES), 1)

    def apply(c, _):
        offset = info_ref[c, 0]
        start = pl.multiple_of(offset // LANES * LANES, LANES)
        c_op = classes - 1 - c if flip else c
        new = dot(op_ref[c_op], picked[:depth, pl.ds(start, 2 * LANES)])
        keep = lane >= offset - start
        for first, part in zip((0, rows), halves(new)):
            at = pl.ds(start, LANES)
            old = out_ref[first : first + rows, at]
            out_ref[first : first + rows, at] = jnp.where(keep, part[:, :LANES], old)
            out_ref[first : first + rows, pl.ds(start + LANES, LANES)] = part[:, LANES:]
        return 0

    lax.fori_loop(first_class, last_class, apply, 0, unroll=UNROLL)


def add_terms(first, info_ref, index_ref, terms_ref, sums):
    def add(part, size):
        lanes = size * CHUNK
        row = part * (CHUNK // LANES)
        hot = hot_columns(index_ref, row, lanes // LANES, first, sums.shape[1])
        at = pl.ds(pl.multiple_of(part * CHUNK, CHUNK), lanes)
        sums[...] += dot_nt(terms_ref[:, at], hot)

    for_parts(info_ref[info_ref.shape[0] - 1, 0], SCATTER_PART, add)


def scatter_kernel(starts, info_ref, index_ref, terms_ref, *refs):
    outs, sums = refs[:-1], refs[-1]
    sums[...] = jnp.zeros_like(sums)
    add_terms(starts[0], info_ref, index_ref, terms_ref, sums)
    rows = sums.shape[0] // 2
    for out, start in zip(outs, starts):
        low = start - starts[0]
        at = slice(low, low + out.shape[1])
        out[...] = sums[: out.shape[0], at] + sums[rows : rows + out.shape[0], at]


def export_kernel(starts, list_row, meta_ref, *refs):
    segs, out_ref = refs[: len(starts)], refs[len(starts)]
    row = meta_ref[list_row : list_row + 1, LANES:]
    out = 0.0
    for seg, first in zip(segs, starts):
        out = out + dot(seg[...], one_hot(row, first, seg.shape[1]))
    out_ref[...] = out.astype(BF16)
    for own in refs[len(starts) + 1 :]:
        own[...] = segs[0][...]


def came_back(first, row, meta_ref, returned, width):
    out = 0.0
    for i, ref in enumerate(returned):
        hot = one_hot(meta_ref[row + i : row + i + 1, LANES:], first, width)
        high, low = halves(ref[...])
        out = out + dot_nt(high, hot) + dot_nt(low, hot)
    return out


def return_kernel(first, row, meta_ref, base_ref, *refs):
    returned, out_ref = refs[:-1], refs[-1]
    out_ref[...] = base_ref[...] + came_back(first, row, meta_ref, returned, out_ref.shape[1])


def local_kernel(
    row, meta_ref, info_ref, target_ref, ahead_ref, source_ref, back_ref, *refs
):
    returned, (out_ref, sums) = refs[:-2], refs[-2:]
    count, rows = out_ref.shape[0], sums.shape[0] // 2
    sums[...] = jnp.zeros_like(sums)
    add_terms(0, info_ref, target_ref, ahead_ref, sums)
    add_terms(0, info_ref, source_ref, back_ref, sums)
    out = came_back(0, row, meta_ref, returned, out_ref.shape[1])
    out_ref[...] = out + (sums[:count, :] + sums[rows : rows + count, :])


def per_device(multipoles, operators, boundary, pair_target, pair_source, pair_count):
    coefficients, cells = multipoles.shape
    cuts, sent = boundary.shape
    classes, width = pair_target.shape
    starts = [0] + [cells + cut * sent for cut in range(cuts)]
    sizes = [cells] + [sent] * cuts
    pool_width = cells + cuts * sent
    rows = up(coefficients, TILE)
    packed = classes * width + 2 * CHUNK + LANES

    index_shape = shape(packed // LANES, LANES, jnp.int32)

    def pick(segments, index, after):
        height = sum(segment.shape[1] for segment in segments)
        return call(
            lambda *refs: pick_kernel(starts, *refs),
            shape(rows, packed, BF16),
            [info, index] + list(segments),
            after,
            limit=16,
            scratch=[pltpu.VMEM((rows, height), BF16)],
            us=4.0,
        )

    def apply(columns, flip, after, first, last, terms=()):
        return call(
            lambda *refs: apply_kernel(flip, first, last, *refs),
            shape(2 * rows, packed, BF16),
            [info, ordered, columns, *terms],
            after,
            limit=8,
            us=0.1,
            input_output_aliases={4: 0} if terms else {},
        )

    def scatter(values, index, first, last, after, us):
        height = sum(sizes[first:last])
        return call(
            lambda *refs: scatter_kernel(starts[first:last], *refs),
            [shape(coefficients, size, F32) for size in sizes[first:last]],
            [info, index, values],
            after,
            limit=8,
            scratch=[pltpu.VMEM((2 * rows, height), F32)],
            us=us,
        )

    segments, returned, sums = [multipoles], [], [None] * (cuts + 1)
    to_source = (cells - 1).bit_length()
    to_count = to_source + (pool_width - 1).bit_length()
    assert to_count < 32
    assert width == sent == LANES and classes >= cuts
    beside = ((0, 0), (0, sent))
    code = jnp.pad(pair_target, beside) | jnp.pad(pair_source, beside) << to_source
    lane = lax.broadcasted_iota(jnp.int32, code.shape, 1)
    code = jnp.where(lane < pair_count, code, -1)
    lists = jnp.pad(boundary, ((0, classes - cuts), (width, 0)))
    meta = jnp.where(lane < width, code, lists)

    def export(after):
        cut = len(segments) - 1
        with jax.named_scope("export"):
            out = [shape(coefficients, sent, BF16)]
            if cut == 0:
                out.append(shape(coefficients, cells, BF16))
            exported, *own = call(
                lambda *refs: export_kernel(starts[: cut + 1], cut, *refs),
                out,
                [meta] + segments,
                after,
            )
            segments[:1] = own or segments[:1]
        segments.append(from_partner(exported, cuts - 1 - cut))
        return exported

    def give_back(after):
        cut = cuts - 1 - len(returned)
        outgoing = sums[cut + 1]
        if returned:
            with jax.named_scope("return"):
                outgoing = call(
                    lambda *refs: return_kernel(starts[cut + 1], cut + 1, *refs),
                    shape(coefficients, sent, F32),
                    [meta, outgoing] + returned,
                    after,
                )
        returned.insert(0, from_partner(outgoing, cuts - 1 - cut))
        return outgoing

    def more_sums(after, us):
        last = max((cut for cut in range(1, cuts + 1) if sums[cut] is None), default=0)
        if last == 0:
            return after
        first = last if last == cuts else max(last - 1, 1)
        with jax.named_scope("reverse_sums"):
            sums[first : last + 1] = scatter(back, sources, first, last + 1, after, us)
        return sums[first]

    step = export(meta)
    with jax.named_scope("pack_slots"):
        targets, sources, info, picked = pl.pallas_call(
            lambda _, *refs: pack_kernel(classes, (to_source, to_count), *refs),
            out_shape=[
                index_shape,
                index_shape,
                shape(classes + 8, LANES, jnp.int32),
                shape(rows, packed, BF16),
            ],
            in_specs=[pl.BlockSpec(memory_space=pl.ANY), VMEM, VMEM],
            out_specs=[VMEM] * 4,
            scratch_shapes=[pltpu.VMEM((rows, cells), BF16)]
            + [pltpu.VMEM((classes, LANES), jnp.int32)] * 2,
            compiler_params=params(8),
            cost_estimate=takes(2.5),
        )(step, meta, segments[0])
    with jax.named_scope("order_operators"):
        ordered = call(
            order_kernel,
            jax.ShapeDtypeStruct((classes, rows, coefficients), BF16),
            [operators.transpose(1, 0, 2)],
            info,
            limit=8,
            us=1.3,
        )
    early = min(16, classes // 2)
    step = export(ordered)
    with jax.named_scope("reverse_terms"):
        back = apply(picked, True, step, 0, early)
    step = export(back) if len(segments) <= cuts else back
    with jax.named_scope("reverse_terms"):
        back = apply(picked, True, step, early, classes, [back])
    step = more_sums(back, 0.1)
    step = give_back(step)
    step = export(step) if len(segments) <= cuts else step
    step = more_sums(step, 4.0)
    step = give_back(step)
    while len(segments) <= cuts:
        step = export(step)
    while any(part is None for part in sums[1:]):
        step = more_sums(step, 4.0)
    step = give_back(step)
    with jax.named_scope("forward_columns"):
        columns = pick(segments, sources, step)
    ends = [classes * part // 4 for part in range(5)]
    ahead, step = [], columns
    for part in range(4):
        after = columns
        if part >= 2 and len(returned) < cuts:
            after = give_back(ahead[0])
        with jax.named_scope("forward_terms"):
            ahead = [apply(columns, False, after, ends[part], ends[part + 1], ahead)]
    (ahead,) = ahead
    step = ahead
    while len(returned) < cuts:
        step = give_back(step)
    with jax.named_scope("local_sums"):
        local = call(
            lambda *refs: local_kernel(1, *refs),
            shape(coefficients, cells, F32),
            [meta, info, targets, ahead, sources, back] + returned[1:],
            step,
            limit=8,
            scratch=[pltpu.VMEM((2 * rows, cells), F32)],
            us=0.1,
        )
    with jax.named_scope("last_sum"):
        return call(
            lambda *refs: return_kernel(0, 0, *refs),
            shape(coefficients, cells, F32),
            [meta, local, returned[0]],
            local,
        )


def solution(mesh):
    split = P(None, AXES)
    return jax.shard_map(
        per_device,
        mesh=mesh,
        in_specs=(split, P(), split, split, split, split),
        out_specs=split,
        check_vma=False,
    )
```

```python
import math

import jax
import jax.numpy as jnp
from jax import lax
from jax.experimental import pallas as pl
from jax.experimental.pallas import tpu as pltpu
from jax.sharding import PartitionSpec as P

LANES = 128
CHUNK = 512
PICK_PART = 8
UNROLL = 16
SCATTER_PART = 8
TILE = 16
AXES = ("gx", "gy")
VMEM = pl.BlockSpec(memory_space=pltpu.VMEM)
BF16 = jnp.bfloat16
F32 = jnp.float32


def up(size, multiple):
    return -(-size // multiple) * multiple


def params(mebibytes):
    return pltpu.CompilerParams(vmem_limit_bytes=mebibytes * 1024 * 1024)


def shape(rows, columns, kind):
    return jax.ShapeDtypeStruct((rows, columns), kind)


def call(kernel, out_shape, args, after, limit=4, scratch=(), us=0.3, **more):
    single = not isinstance(out_shape, (tuple, list))
    return pl.pallas_call(
        lambda _, *refs: kernel(*refs),
        out_shape=out_shape,
        in_specs=[pl.BlockSpec(memory_space=pl.ANY)] + [VMEM] * len(args),
        out_specs=VMEM if single else [VMEM] * len(out_shape),
        scratch_shapes=list(scratch),
        compiler_params=params(limit),
        cost_estimate=takes(us),
        **more,
    )(after, *args)


def takes(us):
    return pl.CostEstimate(flops=int(us * 1e9), bytes_accessed=0, transcendentals=0)


def dot(a, b):
    return jnp.dot(a, b, preferred_element_type=F32)


def dot_nt(a, b):
    return lax.dot_general(a, b, (((1,), (1,)), ((), ())), preferred_element_type=F32)


def halves(wide):
    high = wide.astype(BF16)
    return high, (wide - high.astype(F32)).astype(BF16)


def from_partner(block, distance):
    count = lax.axis_size(AXES)
    route = []
    for low in range(count):
        high = low | 1 << distance
        if high != low and high < count:
            route += [(low, high), (high, low)]
    return lax.ppermute(block, AXES, route)


def one_hot(row, first, height):
    place = lax.broadcasted_iota(jnp.int32, (height, row.shape[1]), 0)
    return jnp.where(place == row - first, 1.0, 0.0).astype(BF16)


def hot_columns(index_ref, row, count, first, height):
    columns = []
    for n in range(count):
        index = index_ref[pl.ds(row + n, 1), :]
        blocks = [
            one_hot(index, first + low, min(LANES, height - low))
            for low in range(0, height, LANES)
        ]
        columns.append(jnp.concatenate(blocks, axis=0))
    return jnp.concatenate(columns, axis=1)


def for_parts(total, largest, body):
    chunks = pl.cdiv(total, CHUNK)
    chunks = jnp.where(lax.rem(chunks, 4) == 3, chunks + 1, chunks)

    def whole(k, _):
        body(k * largest, largest)
        return 0

    lax.fori_loop(0, chunks // largest, whole, 0)
    size = largest // 2
    while size:
        done = chunks // (2 * size) * (2 * size)

        @pl.when(lax.rem(chunks // size, 2) == 1)
        def _(done=done, size=size):
            body(done, size)

        size //= 2


def pick_columns(total, index_ref, pool, picked):
    def pick(first, size):
        lanes = size * CHUNK
        row = first * (CHUNK // LANES)
        hot = hot_columns(index_ref, row, lanes // LANES, 0, pool.shape[1])
        at = pl.ds(pl.multiple_of(first * CHUNK, CHUNK), lanes)
        picked[:, at] = dot(pool[...], hot).astype(BF16)

    for_parts(total, PICK_PART, pick)


def pack_kernel(
    classes, shifts, meta_ref, mult_ref, packed_target, packed_source, info_ref, picked, pool, counts, codes
):
    to_source, to_count = shifts
    codes[...] = meta_ref[:, :LANES]
    slots = jnp.where(codes[...] >= 0, 1, 0)
    counts[...] = jnp.broadcast_to(jnp.sum(slots, axis=1, keepdims=True), slots.shape)
    lane = lax.broadcasted_iota(jnp.int32, (1, LANES), 1)

    def place(c, carry):
        offset, current = carry
        following = offset + counts[c, 0]
        info_ref[pl.ds(c, 1), :] = jnp.full((1, LANES), offset, jnp.int32)
        shift = lax.rem(offset, LANES)
        row = offset // LANES
        turned = pltpu.roll(codes[pl.ds(c, 1), :], shift, 1)
        current = jnp.where(lane >= shift, turned, current)
        packed_target[pl.ds(row, 1), :] = current
        packed_target[pl.ds(row + 1, 1), :] = turned
        return following, jnp.where(following // LANES == row, current, turned)

    none = jnp.zeros((1, LANES), jnp.int32)
    total, _ = lax.fori_loop(0, classes, place, (0, none), unroll=8)
    info_ref[classes:, :] = jnp.full((8, LANES), total, jnp.int32)
    position = lax.broadcasted_iota(jnp.int32, packed_target.shape, 0) * LANES
    position = position + lax.broadcasted_iota(jnp.int32, packed_target.shape, 1)
    used = position < total
    code = packed_target[...]
    source = (code >> to_source) & ((1 << (to_count - to_source)) - 1)
    packed_source[...] = jnp.where(used, source, -1)
    packed_target[...] = jnp.where(used, code & ((1 << to_source) - 1), -1)

    pool[...] = jnp.zeros_like(pool)
    pool[: mult_ref.shape[0], :] = mult_ref[...]
    pick_columns(total, packed_target, pool, picked)


def order_kernel(op_ref, ordered):
    for i in range(0, op_ref.shape[0], TILE):
        size = min(TILE, op_ref.shape[0] - i)
        block = jnp.swapaxes(op_ref[i : i + size], 0, 1)
        ordered[:, i : i + size, :] = block


def pick_kernel(starts, info_ref, index_ref, *refs):
    segs = refs[: len(starts)]
    picked, pool = refs[len(starts) :]
    pool[...] = jnp.zeros_like(pool)
    for seg, first in zip(segs, starts):
        pool[: seg.shape[0], first : first + seg.shape[1]] = seg[...]
    pick_columns(info_ref[info_ref.shape[0] - 1, 0], index_ref, pool, picked)


def apply_kernel(flip, first_class, last_class, info_ref, op_ref, picked, *refs):
    out_ref = refs[-1]
    classes, rows, depth = op_ref.shape
    if first_class == 0:
        last = pl.multiple_of(info_ref[classes, 0] // CHUNK * CHUNK, CHUNK)
        out_ref[:, pl.ds(last, 2 * CHUNK)] = jnp.zeros((2 * rows, 2 * CHUNK), BF16)
    lane = lax.broadcasted_iota(jnp.int32, (rows, LANES), 1)

    def apply(c, _):
        offset = info_ref[c, 0]
        start = pl.multiple_of(offset // LANES * LANES, LANES)
        c_op = classes - 1 - c if flip else c
        new = dot(op_ref[c_op], picked[:depth, pl.ds(start, 2 * LANES)])
        keep = lane >= offset - start
        for first, part in zip((0, rows), halves(new)):
            at = pl.ds(start, LANES)
            old = out_ref[first : first + rows, at]
            out_ref[first : first + rows, at] = jnp.where(keep, part[:, :LANES], old)
            out_ref[first : first + rows, pl.ds(start + LANES, LANES)] = part[:, LANES:]
        return 0

    lax.fori_loop(first_class, last_class, apply, 0, unroll=UNROLL)


def add_terms(first, info_ref, index_ref, terms_ref, sums):
    def add(part, size):
        lanes = size * CHUNK
        row = part * (CHUNK // LANES)
        hot = hot_columns(index_ref, row, lanes // LANES, first, sums.shape[1])
        at = pl.ds(pl.multiple_of(part * CHUNK, CHUNK), lanes)
        sums[...] += dot_nt(terms_ref[:, at], hot)

    for_parts(info_ref[info_ref.shape[0] - 1, 0], SCATTER_PART, add)


def scatter_kernel(starts, info_ref, index_ref, terms_ref, *refs):
    outs, sums = refs[:-1], refs[-1]
    sums[...] = jnp.zeros_like(sums)
    add_terms(starts[0], info_ref, index_ref, terms_ref, sums)
    rows = sums.shape[0] // 2
    for out, start in zip(outs, starts):
        low = start - starts[0]
        at = slice(low, low + out.shape[1])
        out[...] = sums[: out.shape[0], at] + sums[rows : rows + out.shape[0], at]


def export_kernel(starts, list_row, meta_ref, *refs):
    segs, out_ref = refs[: len(starts)], refs[len(starts)]
    row = meta_ref[list_row : list_row + 1, LANES:]
    pool = jnp.concatenate([seg[...] for seg in segs], axis=1)
    out_ref[...] = dot(pool, one_hot(row, 0, pool.shape[1])).astype(BF16)
    for own in refs[len(starts) + 1 :]:
        own[...] = segs[0][...]


def came_back(first, row, meta_ref, returned, width):
    parts, hots = [], []
    for i, ref in enumerate(returned):
        hot = one_hot(meta_ref[row + i : row + i + 1, LANES:], first, width)
        parts += halves(ref[...])
        hots += [hot, hot]
    return dot_nt(jnp.concatenate(parts, axis=1), jnp.concatenate(hots, axis=1))


def return_kernel(first, row, meta_ref, base_ref, *refs):
    returned, out_ref = refs[:-1], refs[-1]
    out_ref[...] = base_ref[...] + came_back(first, row, meta_ref, returned, out_ref.shape[1])


def local_kernel(
    row, meta_ref, info_ref, target_ref, ahead_ref, source_ref, back_ref, *refs
):
    returned, (out_ref, sums) = refs[:-2], refs[-2:]
    count, rows = out_ref.shape[0], sums.shape[0] // 2
    sums[...] = jnp.zeros_like(sums)
    add_terms(0, info_ref, target_ref, ahead_ref, sums)
    add_terms(0, info_ref, source_ref, back_ref, sums)
    out = came_back(0, row, meta_ref, returned, out_ref.shape[1])
    out_ref[...] = out + (sums[:count, :] + sums[rows : rows + count, :])


def per_device(multipoles, operators, boundary, pair_target, pair_source, pair_count):
    coefficients, cells = multipoles.shape
    cuts, sent = boundary.shape
    classes, width = pair_target.shape
    starts = [0] + [cells + cut * sent for cut in range(cuts)]
    sizes = [cells] + [sent] * cuts
    pool_width = cells + cuts * sent
    rows = up(coefficients, TILE)
    packed = classes * width + 2 * CHUNK + LANES

    index_shape = shape(packed // LANES, LANES, jnp.int32)

    def pick(segments, index, after):
        height = sum(segment.shape[1] for segment in segments)
        return call(
            lambda *refs: pick_kernel(starts, *refs),
            shape(rows, packed, BF16),
            [info, index] + list(segments),
            after,
            limit=16,
            scratch=[pltpu.VMEM((rows, height), BF16)],
            us=4.0,
        )

    def apply(columns, flip, after, first, last, terms=()):
        return call(
            lambda *refs: apply_kernel(flip, first, last, *refs),
            shape(2 * rows, packed, BF16),
            [info, ordered, columns, *terms],
            after,
            limit=8,
            us=0.1,
            input_output_aliases={4: 0} if terms else {},
        )

    def scatter(values, index, first, last, after, us):
        height = sum(sizes[first:last])
        return call(
            lambda *refs: scatter_kernel(starts[first:last], *refs),
            [shape(coefficients, size, F32) for size in sizes[first:last]],
            [info, index, values],
            after,
            limit=8,
            scratch=[pltpu.VMEM((2 * rows, height), F32)],
            us=us,
        )

    segments, returned, sums = [multipoles], [], [None] * (cuts + 1)
    to_source = (cells - 1).bit_length()
    to_count = to_source + (pool_width - 1).bit_length()
    assert to_count < 32
    assert width == sent == LANES and classes >= cuts
    beside = ((0, 0), (0, sent))
    code = jnp.pad(pair_target, beside) | jnp.pad(pair_source, beside) << to_source
    lane = lax.broadcasted_iota(jnp.int32, code.shape, 1)
    code = jnp.where(lane < pair_count, code, -1)
    lists = jnp.pad(boundary, ((0, classes - cuts), (width, 0)))
    meta = jnp.where(lane < width, code, lists)

    def export(after):
        cut = len(segments) - 1
        with jax.named_scope("export"):
            out = [shape(coefficients, sent, BF16)]
            if cut == 0:
                out.append(shape(coefficients, cells, BF16))
            exported, *own = call(
                lambda *refs: export_kernel(starts[: cut + 1], cut, *refs),
                out,
                [meta] + segments,
                after,
            )
            segments[:1] = own or segments[:1]
        segments.append(from_partner(exported, cuts - 1 - cut))
        return exported

    def give_back(after):
        cut = cuts - 1 - len(returned)
        outgoing = sums[cut + 1]
        if returned:
            with jax.named_scope("return"):
                outgoing = call(
                    lambda *refs: return_kernel(starts[cut + 1], cut + 1, *refs),
                    shape(coefficients, sent, F32),
                    [meta, outgoing] + returned,
                    after,
                )
        returned.insert(0, from_partner(outgoing, cuts - 1 - cut))
        return outgoing

    def more_sums(after, us):
        last = max((cut for cut in range(1, cuts + 1) if sums[cut] is None), default=0)
        if last == 0:
            return after
        first = last if last == cuts else max(last - 1, 1)
        with jax.named_scope("reverse_sums"):
            sums[first : last + 1] = scatter(back, sources, first, last + 1, after, us)
        return sums[first]

    step = export(meta)
    with jax.named_scope("pack_slots"):
        targets, sources, info, picked = pl.pallas_call(
            lambda _, *refs: pack_kernel(classes, (to_source, to_count), *refs),
            out_shape=[
                index_shape,
                index_shape,
                shape(classes + 8, LANES, jnp.int32),
                shape(rows, packed, BF16),
            ],
            in_specs=[pl.BlockSpec(memory_space=pl.ANY), VMEM, VMEM],
            out_specs=[VMEM] * 4,
            scratch_shapes=[pltpu.VMEM((rows, cells), BF16)]
            + [pltpu.VMEM((classes, LANES), jnp.int32)] * 2,
            compiler_params=params(8),
            cost_estimate=takes(2.5),
        )(step, meta, segments[0])
    with jax.named_scope("order_operators"):
        ordered = call(
            order_kernel,
            jax.ShapeDtypeStruct((classes, rows, coefficients), BF16),
            [operators.transpose(1, 0, 2)],
            info,
            limit=8,
            us=1.3,
        )
    early = min(16, classes // 2)
    step = export(ordered)
    with jax.named_scope("reverse_terms"):
        back = apply(picked, True, step, 0, early)
    step = export(back) if len(segments) <= cuts else back
    with jax.named_scope("reverse_terms"):
        back = apply(picked, True, step, early, classes, [back])
    step = more_sums(back, 0.1)
    step = give_back(step)
    step = export(step) if len(segments) <= cuts else step
    step = more_sums(step, 4.0)
    step = give_back(step)
    while len(segments) <= cuts:
        step = export(step)
    while any(part is None for part in sums[1:]):
        step = more_sums(step, 4.0)
    step = give_back(step)
    with jax.named_scope("forward_columns"):
        columns = pick(segments, sources, step)
    ends = [classes * part // 4 for part in range(5)]
    ahead, step = [], columns
    for part in range(4):
        after = columns
        if part >= 2 and len(returned) < cuts:
            after = give_back(ahead[0])
        with jax.named_scope("forward_terms"):
            ahead = [apply(columns, False, after, ends[part], ends[part + 1], ahead)]
    (ahead,) = ahead
    step = ahead
    while len(returned) < cuts:
        step = give_back(step)
    with jax.named_scope("local_sums"):
        local = call(
            lambda *refs: local_kernel(1, *refs),
            shape(coefficients, cells, F32),
            [meta, info, targets, ahead, sources, back] + returned[1:],
            step,
            limit=8,
            scratch=[pltpu.VMEM((2 * rows, cells), F32)],
            us=0.1,
        )
    with jax.named_scope("last_sum"):
        return call(
            lambda *refs: return_kernel(0, 0, *refs),
            shape(coefficients, cells, F32),
            [meta, local, returned[0]],
            local,
        )


def solution(mesh):
    split = P(None, AXES)
    return jax.shard_map(
        per_device,
        mesh=mesh,
        in_specs=(split, P(), split, split, split, split),
        out_specs=split,
        check_vma=False,
    )
```

```python
import math

import jax
import jax.numpy as jnp
from jax import lax
from jax.experimental import pallas as pl
from jax.experimental.pallas import tpu as pltpu
from jax.sharding import PartitionSpec as P

LANES = 128
CHUNK = 512
PICK_PART = 8
UNROLL = 16
SCATTER_PART = 8
TILE = 16
AXES = ("gx", "gy")
VMEM = pl.BlockSpec(memory_space=pltpu.VMEM)
BF16 = jnp.bfloat16
F32 = jnp.float32


def up(size, multiple):
    return -(-size // multiple) * multiple


def params(mebibytes):
    return pltpu.CompilerParams(vmem_limit_bytes=mebibytes * 1024 * 1024)


def shape(rows, columns, kind):
    return jax.ShapeDtypeStruct((rows, columns), kind)


def call(kernel, out_shape, args, after, limit=4, scratch=(), us=0.3, **more):
    single = not isinstance(out_shape, (tuple, list))
    return pl.pallas_call(
        lambda _, *refs: kernel(*refs),
        out_shape=out_shape,
        in_specs=[pl.BlockSpec(memory_space=pl.ANY)] + [VMEM] * len(args),
        out_specs=VMEM if single else [VMEM] * len(out_shape),
        scratch_shapes=list(scratch),
        compiler_params=params(limit),
        cost_estimate=takes(us),
        **more,
    )(after, *args)


def takes(us):
    return pl.CostEstimate(flops=int(us * 1e9), bytes_accessed=0, transcendentals=0)


def dot(a, b):
    return jnp.dot(a, b, preferred_element_type=F32)


def dot_nt(a, b):
    return lax.dot_general(a, b, (((1,), (1,)), ((), ())), preferred_element_type=F32)


def halves(wide):
    high = wide.astype(BF16)
    return high, (wide - high.astype(F32)).astype(BF16)


def from_partner(block, distance):
    count = lax.axis_size(AXES)
    route = []
    for low in range(count):
        high = low | 1 << distance
        if high != low and high < count:
            route += [(low, high), (high, low)]
    return lax.ppermute(block, AXES, route)


def one_hot(row, first, height):
    place = lax.broadcasted_iota(jnp.int32, (height, row.shape[1]), 0)
    return jnp.where(place == row - first, 1.0, 0.0).astype(BF16)


def hot_columns(index_ref, row, count, first, height):
    columns = []
    for n in range(count):
        index = index_ref[pl.ds(row + n, 1), :]
        blocks = [
            one_hot(index, first + low, min(LANES, height - low))
            for low in range(0, height, LANES)
        ]
        columns.append(jnp.concatenate(blocks, axis=0))
    return jnp.concatenate(columns, axis=1)


def for_parts(total, largest, body):
    chunks = pl.cdiv(total, CHUNK)
    chunks = jnp.where(lax.rem(chunks, 4) == 3, chunks + 1, chunks)

    def whole(k, _):
        body(k * largest, largest)
        return 0

    lax.fori_loop(0, chunks // largest, whole, 0)
    size = largest // 2
    while size:
        done = chunks // (2 * size) * (2 * size)

        @pl.when(lax.rem(chunks // size, 2) == 1)
        def _(done=done, size=size):
            body(done, size)

        size //= 2


def pick_columns(total, index_ref, pool, picked):
    def pick(first, size):
        lanes = size * CHUNK
        row = first * (CHUNK // LANES)
        hot = hot_columns(index_ref, row, lanes // LANES, 0, pool.shape[1])
        at = pl.ds(pl.multiple_of(first * CHUNK, CHUNK), lanes)
        picked[:, at] = dot(pool[...], hot).astype(BF16)

    for_parts(total, PICK_PART, pick)


def pack_kernel(
    classes, shifts, meta_ref, mult_ref, packed_target, packed_source, info_ref, picked, pool, counts, codes
):
    to_source, to_count = shifts
    codes[...] = meta_ref[:, :LANES]
    slots = jnp.where(codes[...] >= 0, 1, 0)
    counts[...] = jnp.broadcast_to(jnp.sum(slots, axis=1, keepdims=True), slots.shape)
    lane = lax.broadcasted_iota(jnp.int32, (1, LANES), 1)

    def place(c, carry):
        offset, current = carry
        following = offset + counts[c, 0]
        info_ref[pl.ds(c, 1), :] = jnp.full((1, LANES), offset, jnp.int32)
        shift = lax.rem(offset, LANES)
        row = offset // LANES
        turned = pltpu.roll(codes[pl.ds(c, 1), :], shift, 1)
        current = jnp.where(lane >= shift, turned, current)
        packed_target[pl.ds(row, 1), :] = current
        packed_target[pl.ds(row + 1, 1), :] = turned
        return following, jnp.where(following // LANES == row, current, turned)

    none = jnp.zeros((1, LANES), jnp.int32)
    total, _ = lax.fori_loop(0, classes, place, (0, none), unroll=32)
    info_ref[classes:, :] = jnp.full((8, LANES), total, jnp.int32)
    position = lax.broadcasted_iota(jnp.int32, packed_target.shape, 0) * LANES
    position = position + lax.broadcasted_iota(jnp.int32, packed_target.shape, 1)
    used = position < total
    code = packed_target[...]
    source = (code >> to_source) & ((1 << (to_count - to_source)) - 1)
    packed_source[...] = jnp.where(used, source, -1)
    packed_target[...] = jnp.where(used, code & ((1 << to_source) - 1), -1)

    pool[...] = jnp.zeros_like(pool)
    pool[: mult_ref.shape[0], :] = mult_ref[...]
    pick_columns(total, packed_target, pool, picked)


def order_kernel(op_ref, ordered):
    for i in range(0, op_ref.shape[0], TILE):
        size = min(TILE, op_ref.shape[0] - i)
        block = jnp.swapaxes(op_ref[i : i + size], 0, 1)
        ordered[:, i : i + size, :] = block


def pick_kernel(starts, info_ref, index_ref, *refs):
    segs = refs[: len(starts)]
    picked, pool = refs[len(starts) :]
    pool[...] = jnp.zeros_like(pool)
    for seg, first in zip(segs, starts):
        pool[: seg.shape[0], first : first + seg.shape[1]] = seg[...]
    pick_columns(info_ref[info_ref.shape[0] - 1, 0], index_ref, pool, picked)


def apply_kernel(flip, first_class, last_class, info_ref, op_ref, picked, *refs):
    out_ref = refs[-1]
    classes, rows, depth = op_ref.shape
    if first_class == 0:
        last = pl.multiple_of(info_ref[classes, 0] // CHUNK * CHUNK, CHUNK)
        out_ref[:, pl.ds(last, 2 * CHUNK)] = jnp.zeros((2 * rows, 2 * CHUNK), BF16)
    lane = lax.broadcasted_iota(jnp.int32, (rows, LANES), 1)

    def apply(c, _):
        offset = info_ref[c, 0]
        start = pl.multiple_of(offset // LANES * LANES, LANES)
        c_op = classes - 1 - c if flip else c
        new = dot(op_ref[c_op], picked[:depth, pl.ds(start, 2 * LANES)])
        keep = lane >= offset - start
        for first, part in zip((0, rows), halves(new)):
            at = pl.ds(start, LANES)
            old = out_ref[first : first + rows, at]
            out_ref[first : first + rows, at] = jnp.where(keep, part[:, :LANES], old)
            out_ref[first : first + rows, pl.ds(start + LANES, LANES)] = part[:, LANES:]
        return 0

    lax.fori_loop(first_class, last_class, apply, 0, unroll=UNROLL)


def add_terms(first, info_ref, index_ref, terms_ref, sums):
    def add(part, size):
        lanes = size * CHUNK
        row = part * (CHUNK // LANES)
        hot = hot_columns(index_ref, row, lanes // LANES, first, sums.shape[1])
        at = pl.ds(pl.multiple_of(part * CHUNK, CHUNK), lanes)
        sums[...] += dot_nt(terms_ref[:, at], hot)

    for_parts(info_ref[info_ref.shape[0] - 1, 0], SCATTER_PART, add)


def scatter_kernel(starts, info_ref, index_ref, terms_ref, *refs):
    outs, sums = refs[:-1], refs[-1]
    sums[...] = jnp.zeros_like(sums)
    add_terms(starts[0], info_ref, index_ref, terms_ref, sums)
    rows = sums.shape[0] // 2
    for out, start in zip(outs, starts):
        low = start - starts[0]
        at = slice(low, low + out.shape[1])
        out[...] = sums[: out.shape[0], at] + sums[rows : rows + out.shape[0], at]


def export_kernel(starts, list_row, meta_ref, *refs):
    segs, out_ref = refs[: len(starts)], refs[len(starts)]
    row = meta_ref[list_row : list_row + 1, LANES:]
    pool = jnp.concatenate([seg[...] for seg in segs], axis=1)
    out_ref[...] = dot(pool, one_hot(row, 0, pool.shape[1])).astype(BF16)
    for own in refs[len(starts) + 1 :]:
        own[...] = segs[0][...]


def came_back(first, row, meta_ref, returned, width):
    parts, hots = [], []
    for i, ref in enumerate(returned):
        hot = one_hot(meta_ref[row + i : row + i + 1, LANES:], first, width)
        parts += halves(ref[...])
        hots += [hot, hot]
    return dot_nt(jnp.concatenate(parts, axis=1), jnp.concatenate(hots, axis=1))


def return_kernel(first, row, meta_ref, base_ref, *refs):
    returned, out_ref = refs[:-1], refs[-1]
    out_ref[...] = base_ref[...] + came_back(first, row, meta_ref, returned, out_ref.shape[1])


def local_kernel(
    row, meta_ref, info_ref, target_ref, ahead_ref, source_ref, back_ref, *refs
):
    returned, (out_ref, sums) = refs[:-2], refs[-2:]
    count, rows = out_ref.shape[0], sums.shape[0] // 2
    sums[...] = jnp.zeros_like(sums)
    add_terms(0, info_ref, target_ref, ahead_ref, sums)
    add_terms(0, info_ref, source_ref, back_ref, sums)
    out = came_back(0, row, meta_ref, returned, out_ref.shape[1])
    out_ref[...] = out + (sums[:count, :] + sums[rows : rows + count, :])


def per_device(multipoles, operators, boundary, pair_target, pair_source, pair_count):
    coefficients, cells = multipoles.shape
    cuts, sent = boundary.shape
    classes, width = pair_target.shape
    starts = [0] + [cells + cut * sent for cut in range(cuts)]
    sizes = [cells] + [sent] * cuts
    pool_width = cells + cuts * sent
    rows = up(coefficients, TILE)
    packed = classes * width + 2 * CHUNK + LANES

    index_shape = shape(packed // LANES, LANES, jnp.int32)

    def pick(segments, index, after):
        height = sum(segment.shape[1] for segment in segments)
        return call(
            lambda *refs: pick_kernel(starts, *refs),
            shape(rows, packed, BF16),
            [info, index] + list(segments),
            after,
            limit=16,
            scratch=[pltpu.VMEM((rows, height), BF16)],
            us=4.0,
        )

    def apply(columns, flip, after, first, last, terms=()):
        return call(
            lambda *refs: apply_kernel(flip, first, last, *refs),
            shape(2 * rows, packed, BF16),
            [info, ordered, columns, *terms],
            after,
            limit=8,
            us=0.1,
            input_output_aliases={4: 0} if terms else {},
        )

    def scatter(values, index, first, last, after, us):
        height = sum(sizes[first:last])
        return call(
            lambda *refs: scatter_kernel(starts[first:last], *refs),
            [shape(coefficients, size, F32) for size in sizes[first:last]],
            [info, index, values],
            after,
            limit=8,
            scratch=[pltpu.VMEM((2 * rows, height), F32)],
            us=us,
        )

    segments, returned, sums = [multipoles], [], [None] * (cuts + 1)
    to_source = (cells - 1).bit_length()
    to_count = to_source + (pool_width - 1).bit_length()
    assert to_count < 32
    assert width == sent == LANES and classes >= cuts
    beside = ((0, 0), (0, sent))
    code = jnp.pad(pair_target, beside) | jnp.pad(pair_source, beside) << to_source
    lane = lax.broadcasted_iota(jnp.int32, code.shape, 1)
    code = jnp.where(lane < pair_count, code, -1)
    lists = jnp.pad(boundary, ((0, classes - cuts), (width, 0)))
    meta = jnp.where(lane < width, code, lists)

    def export(after):
        cut = len(segments) - 1
        with jax.named_scope("export"):
            out = [shape(coefficients, sent, BF16)]
            if cut == 0:
                out.append(shape(coefficients, cells, BF16))
            exported, *own = call(
                lambda *refs: export_kernel(starts[: cut + 1], cut, *refs),
                out,
                [meta] + segments,
                after,
            )
            segments[:1] = own or segments[:1]
        segments.append(from_partner(exported, cuts - 1 - cut))
        return exported

    def give_back(after):
        cut = cuts - 1 - len(returned)
        outgoing = sums[cut + 1]
        if returned:
            with jax.named_scope("return"):
                outgoing = call(
                    lambda *refs: return_kernel(starts[cut + 1], cut + 1, *refs),
                    shape(coefficients, sent, F32),
                    [meta, outgoing] + returned,
                    after,
                )
        returned.insert(0, from_partner(outgoing, cuts - 1 - cut))
        return outgoing

    def more_sums(after, us):
        last = max((cut for cut in range(1, cuts + 1) if sums[cut] is None), default=0)
        if last == 0:
            return after
        first = last if last == cuts else max(last - 1, 1)
        with jax.named_scope("reverse_sums"):
            sums[first : last + 1] = scatter(back, sources, first, last + 1, after, us)
        return sums[first]

    step = export(meta)
    with jax.named_scope("pack_slots"):
        targets, sources, info, picked = pl.pallas_call(
            lambda _, *refs: pack_kernel(classes, (to_source, to_count), *refs),
            out_shape=[
                index_shape,
                index_shape,
                shape(classes + 8, LANES, jnp.int32),
                shape(rows, packed, BF16),
            ],
            in_specs=[pl.BlockSpec(memory_space=pl.ANY), VMEM, VMEM],
            out_specs=[VMEM] * 4,
            scratch_shapes=[pltpu.VMEM((rows, cells), BF16)]
            + [pltpu.VMEM((classes, LANES), jnp.int32)] * 2,
            compiler_params=params(8),
            cost_estimate=takes(2.5),
        )(step, meta, segments[0])
    with jax.named_scope("order_operators"):
        ordered = call(
            order_kernel,
            jax.ShapeDtypeStruct((classes, rows, coefficients), BF16),
            [operators.transpose(1, 0, 2)],
            info,
            limit=8,
            us=1.3,
        )
    early = min(16, classes // 2)
    step = export(ordered)
    with jax.named_scope("reverse_terms"):
        back = apply(picked, True, step, 0, early)
    step = export(back) if len(segments) <= cuts else back
    with jax.named_scope("reverse_terms"):
        back = apply(picked, True, step, early, classes, [back])
    step = more_sums(back, 0.1)
    step = give_back(step)
    step = export(step) if len(segments) <= cuts else step
    step = more_sums(step, 4.0)
    step = give_back(step)
    while len(segments) <= cuts:
        step = export(step)
    while any(part is None for part in sums[1:]):
        step = more_sums(step, 4.0)
    step = give_back(step)
    with jax.named_scope("forward_columns"):
        columns = pick(segments, sources, step)
    ends = [classes * part // 4 for part in range(5)]
    ahead, step = [], columns
    for part in range(4):
        after = columns
        if part >= 2 and len(returned) < cuts:
            after = give_back(ahead[0])
        with jax.named_scope("forward_terms"):
            ahead = [apply(columns, False, after, ends[part], ends[part + 1], ahead)]
    (ahead,) = ahead
    step = ahead
    while len(returned) < cuts:
        step = give_back(step)
    with jax.named_scope("local_sums"):
        local = call(
            lambda *refs: local_kernel(1, *refs),
            shape(coefficients, cells, F32),
            [meta, info, targets, ahead, sources, back] + returned[1:],
            step,
            limit=8,
            scratch=[pltpu.VMEM((2 * rows, cells), F32)],
            us=0.1,
        )
    with jax.named_scope("last_sum"):
        return call(
            lambda *refs: return_kernel(0, 0, *refs),
            shape(coefficients, cells, F32),
            [meta, local, returned[0]],
            local,
        )


def solution(mesh):
    split = P(None, AXES)
    return jax.shard_map(
        per_device,
        mesh=mesh,
        in_specs=(split, P(), split, split, split, split),
        out_specs=split,
        check_vma=False,
    )
```
